128 devices in a mesh: row: 16 (over z_lo, x, core), col: 8 (over z_hi, y).
Axes of the slice: x: 4, y: 4, z: 4 (z_hi: 2, z_lo: 2; z = z_hi * 2 + z_lo), core: 2. Of those that a mesh axis runs over, the one named last changes fastest.
Arguments:
- queries: bfloat16 [256, 512, 1024], P('row', 'col'), may hold values from -6.5 to 6.5
- keys: bfloat16 [256, 512, 1024], P('row', 'col'), may hold values from -6.5 to 6.5
- values: bfloat16 [256, 512, 1024], P('row', 'col'), may hold values from -6 to 6
- grad_output: bfloat16 [256, 512, 1024], P('row', 'col'), may hold values from -6 to 6
Outputs:
- attended: bfloat16 [256, 512, 1024], P('row', 'col')
- query_grad: bfloat16 [256, 512, 1024], P('row', 'col')
- key_grad: bfloat16 [256, 512, 1024], P('row', 'col')
- value_grad: bfloat16 [256, 512, 1024], P('row', 'col')
The draws below stay inside these ranges and needn't reach their ends.
All inputs are finite; a program needn't handle non-finite values.
Results may differ from the reference program's by a relative error of at most 0.0059.
Values may be sent and summed in bfloat16 or wider, within the bound.
A program may use at most 192 MiB of HBM per device.

```python
import jax
import jax.numpy as jnp
from jax import lax

HEAD_DIM = 64
D = 1024
ROWS = 256
COLS = 512


def draw_queries(key, part):
    key = jax.random.fold_in(key, 1)
    result = jnp.clip(jax.random.normal(key, (ROWS, COLS, D), jnp.float32), -6.0, 6.0)
    return result.astype(jnp.bfloat16)


def draw_keys(key, part):
    key = jax.random.fold_in(key, 2)
    result = jnp.clip(jax.random.normal(key, (ROWS, COLS, D), jnp.float32), -6.0, 6.0)
    return result.astype(jnp.bfloat16)


def block_levels(own_key, extent, pieces, least, largest):
    factor_of = 1.0
    for axis_at, blocks in pieces:
        steps = jax.random.uniform(jax.random.fold_in(jax.random.fold_in(own_key, 6), axis_at), (blocks,), jnp.float32, least / len(pieces), largest / len(pieces))
        factor_of = factor_of * jnp.repeat(jnp.exp(steps), extent[axis_at] // blocks).reshape((-1,) + (1,) * (len(extent) - 1 - axis_at))
    return factor_of


def normal_values(own_key, shape, scale, limit, pieces=(), dtype=jnp.bfloat16):
    level = block_levels(own_key, shape, pieces, -0.22, 0.18) if pieces else 1.0
    entries = jax.random.normal(own_key, shape, jnp.float32) * scale * level
    return jnp.minimum(jnp.maximum(entries, -limit), limit).astype(dtype)


def setup_inputs(seed: int = 0) -> dict:
    arg_keys = jax.random.split(jax.random.key(seed), 5)
    queries = draw_queries(jax.random.fold_in(arg_keys[4], 71), 0)
    keys = draw_keys(jax.random.fold_in(arg_keys[4], 71), 0)
    values = normal_values(arg_keys[2], (ROWS, COLS, D), 1.0, 6.0, ((0, 16), (1, 8)))
    grad_output = normal_values(arg_keys[3], (ROWS, COLS, D), 1.0, 6.0, ((0, 16), (1, 8)))
    return dict(queries=queries, keys=keys, values=values, grad_output=grad_output)


def causal_mask(count_q, count_k):
    query_pos = lax.broadcasted_iota(jnp.int32, (count_q, count_k), 0)
    key_pos = lax.broadcasted_iota(jnp.int32, (count_q, count_k), 1)
    return key_pos <= query_pos


def attend_exact(query, key, value, grad_out, allowed):
    query = query.astype(jnp.float32)
    key = key.astype(jnp.float32)
    value = value.astype(jnp.float32)
    grad_out = grad_out.astype(jnp.float32)
    score_scale = query.shape[-1] ** -0.5
    scores = jnp.einsum("bqhd,bkhd->bhqk", query, key) * score_scale
    scores = jnp.where(allowed, scores, -1e30)
    row_max = jnp.max(scores, axis=-1, keepdims=True)
    weights = jnp.exp(scores - row_max)
    probs = weights / jnp.sum(weights, axis=-1, keepdims=True)
    probs_low = lax.optimization_barrier(probs.astype(jnp.bfloat16)).astype(jnp.float32)
    attended = jnp.einsum("bhqk,bkhd->bqhd", probs_low, value)
    dprobs = jnp.einsum("bqhd,bkhd->bhqk", grad_out, value)
    row_delta = jnp.sum(probs * dprobs, axis=-1, keepdims=True)
    dscores = lax.optimization_barrier((probs * (dprobs - row_delta)).astype(jnp.bfloat16)).astype(jnp.float32)
    dquery = jnp.einsum("bhqk,bkhd->bqhd", dscores, key) * score_scale
    key_grad = jnp.einsum("bhqk,bqhd->bkhd", dscores, query) * score_scale
    value_grad = jnp.einsum("bhqk,bqhd->bkhd", probs_low, grad_out)
    return attended, dquery, key_grad, value_grad


def split_heads(array):
    return array.reshape(array.shape[:-1] + (array.shape[-1] // HEAD_DIM, HEAD_DIM))


def merge_heads(array):
    return array.reshape(array.shape[:-2] + (array.shape[-2] * array.shape[-1],))


def reference(queries, keys, values, grad_output):
    half_width = D // 2
    inputs = (queries, keys, values, grad_output)
    row_inputs = tuple(split_heads(item[:, :, :half_width]) for item in inputs)
    col_inputs = tuple(split_heads(item[:, :, half_width:]) for item in inputs)
    allowed_row = causal_mask(COLS, COLS)
    allowed_col = causal_mask(ROWS, ROWS)

    def one_row(items):
        batched = tuple(item[None] for item in items)
        results = attend_exact(batched[0], batched[1], batched[2], batched[3], allowed_row)
        return tuple(result[0] for result in results)

    def one_column(items):
        batched = tuple(item[None] for item in items)
        results = attend_exact(batched[0], batched[1], batched[2], batched[3], allowed_col)
        return tuple(result[0] for result in results)

    row_results = lax.map(one_row, row_inputs)
    col_moved = tuple(jnp.swapaxes(item, 0, 1) for item in col_inputs)
    col_results = tuple(jnp.swapaxes(item, 0, 1) for item in lax.map(one_column, col_moved))
    joined = tuple(
        jnp.concatenate([merge_heads(first), merge_heads(second)], axis=2).astype(jnp.bfloat16)
        for first, second in zip(row_results, col_results)
    )
    return (joined[0], joined[1], joined[2], joined[3])
```

```python
import functools

import jax
import jax.numpy as jnp
from jax import lax
from jax.experimental import pallas as pl
from jax.experimental.pallas import tpu as pltpu
from jax.sharding import PartitionSpec as P

MESH = pl.DeviceIdType.MESH
STEPS = 4
LANES = 128
HALF = 512
ROWS_HERE = 16
COLS_HERE = 64
ROW_SEQ = 256
COL_SEQ = 128
COL_BLOCK = 32
ROW_STEP = ROWS_HERE // STEPS
COL_STEP = COL_BLOCK // STEPS
NT = (((1,), (1,)), ((), ()))
TN = (((0,), (0,)), ((), ()))
NN = (((1,), (0,)), ((), ()))


def dot(a, b, dims):
    return lax.dot_general(a, b, dims, preferred_element_type=jnp.float32)


def attend(q, k, v, g, k_low, v_low):
    length = q.shape[0]
    lane = lax.broadcasted_iota(jnp.int32, (1, LANES), 1)
    allowed = lax.broadcasted_iota(jnp.int32, (length, length), 1) <= lax.broadcasted_iota(
        jnp.int32, (length, length), 0
    )
    zero = jnp.zeros((), jnp.bfloat16)
    q = q * jnp.bfloat16(0.125)
    totals = None
    for head in range(2):
        mine = (lane < 64) if head == 0 else (lane >= 64)
        qh, kh, vh, gh = [jnp.where(mine, t, zero) for t in (q, k, v, g)]
        scores = jnp.where(allowed, dot(qh, k, NT), -1e30)
        dprobs = dot(gh, v, NT)
        top = jnp.max(scores, axis=1, keepdims=True)
        if k_low is not None:
            scores_low = dot(qh, k_low, NT)
            dprobs_low = dot(gh, v_low, NT)
            top = jnp.maximum(top, jnp.max(scores_low, axis=1, keepdims=True))
        weights = jnp.exp(scores - top)
        norm = jnp.sum(weights, axis=1, keepdims=True)
        if k_low is not None:
            weights_low = jnp.exp(scores_low - top)
            norm = norm + jnp.sum(weights_low, axis=1, keepdims=True)
        inverse = 1.0 / norm
        probs = weights * inverse
        delta = jnp.sum(probs * dprobs, axis=1, keepdims=True)
        if k_low is not None:
            probs_low = weights_low * inverse
            delta = delta + jnp.sum(probs_low * dprobs_low, axis=1, keepdims=True)
        ds = (probs * (dprobs - delta)).astype(jnp.bfloat16)
        pb = probs.astype(jnp.bfloat16)
        parts = [dot(pb, vh, NN), dot(ds, kh, NN), dot(ds, qh, TN), dot(pb, gh, TN)]
        if k_low is not None:
            ds_low = (probs_low * (dprobs_low - delta)).astype(jnp.bfloat16)
            pb_low = probs_low.astype(jnp.bfloat16)
            kh_low, vh_low = [jnp.where(mine, t, zero) for t in (k_low, v_low)]
            parts[0] = parts[0] + dot(pb_low, vh_low, NN)
            parts[1] = parts[1] + dot(ds_low, kh_low, NN)
            parts += [dot(ds_low, qh, TN), dot(pb_low, gh, TN)]
        totals = parts if totals is None else [a + b for a, b in zip(totals, parts)]
    totals[1] = totals[1] * 0.125
    return totals


def body(
    q_ref, k_ref, v_ref, g_ref, raw_row, raw_col,
    row_in, row_low, row_out, row_part, row_keep,
    col_in, col_low, col_out, col_part, col_keep,
    stage, send,
    ri_s, ri_r, ri_l, ci_s, ci_r, ci_l,
    ro_s, ro_r, ro_l, co_s, co_r, co_l,
    rf_s, rf_r, cf_s, cf_r, st_l,
):
    inputs = (q_ref, k_ref, v_ref, g_ref)
    row, col = lax.axis_index("row"), lax.axis_index("col")
    z_lo, xc = row // 8, row % 8
    x, core = xc // 2, xc % 2
    z_hi, y = col // 4, col % 4

    def row_peer(d):
        other = (y + d) % 4
        return other, (row, z_hi * 4 + other)

    def col_peer(d):
        other = (xc + d) % 8
        return other, (z_lo * 8 + other, col)

    row_partner = (row, (1 - z_hi) * 4 + y)
    col_partner = ((1 - z_lo) * 8 + xc, col)

    for a in range(4):
        pltpu.make_async_copy(inputs[a].at[:, :, pl.ds(HALF, HALF)], stage.at[a], st_l.at[a]).start()

    barrier = pltpu.get_barrier_semaphore()
    everyone = [row_peer(d)[1] for d in range(1, 4)] + [col_peer(d)[1] for d in range(1, 8)]
    everyone += [row_partner, col_partner]
    for device in everyone:
        pl.semaphore_signal(barrier, inc=1, device_id=device, device_id_type=MESH)
    pl.semaphore_wait(barrier, len(everyone))

    def lanes(i):
        return pl.ds(pl.multiple_of(i * LANES, LANES), LANES)

    def row_in_copy(i, a, d):
        other, device = row_peer(d)
        return pltpu.make_async_remote_copy(
            inputs[a].at[pl.ds(i * ROW_STEP, ROW_STEP), :, lanes(other)],
            row_in.at[a, pl.ds(i * ROW_STEP, ROW_STEP), pl.ds(y * COLS_HERE, COLS_HERE)],
            ri_s.at[i, a, d - 1], ri_r.at[i, a, d - 1], device_id=device, device_id_type=MESH,
        )

    def row_in_own(i, a):
        return pltpu.make_async_copy(
            inputs[a].at[pl.ds(i * ROW_STEP, ROW_STEP), :, lanes(y)],
            row_in.at[a, pl.ds(i * ROW_STEP, ROW_STEP), pl.ds(y * COLS_HERE, COLS_HERE)],
            ri_l.at[i, a],
        )

    def row_in_arrival(i, a, d):
        src = (y + 4 - d) % 4
        place = row_in.at[a, pl.ds(i * ROW_STEP, ROW_STEP), pl.ds(src * COLS_HERE, COLS_HERE)]
        return pltpu.make_async_remote_copy(
            place, place, ri_s.at[i, a, d - 1], ri_r.at[i, a, d - 1],
            device_id=row_peer(d)[1], device_id_type=MESH,
        )

    def col_in_copy(i, d):
        other, device = col_peer(d)
        return pltpu.make_async_remote_copy(
            send.at[:, pl.ds((other % 2) * COL_BLOCK + i * COL_STEP, COL_STEP), :, lanes(other // 2)],
            col_in.at[:, pl.ds(i * COL_STEP, COL_STEP), pl.ds(xc * ROWS_HERE, ROWS_HERE)],
            ci_s.at[i, d - 1], ci_r.at[i, d - 1], device_id=device, device_id_type=MESH,
        )

    def col_in_own(i):
        return pltpu.make_async_copy(
            send.at[:, pl.ds(core * COL_BLOCK + i * COL_STEP, COL_STEP), :, lanes(x)],
            col_in.at[:, pl.ds(i * COL_STEP, COL_STEP), pl.ds(xc * ROWS_HERE, ROWS_HERE)],
            ci_l.at[i],
        )

    def col_in_arrival(i, d):
        src = (xc + 8 - d) % 8
        place = col_in.at[:, pl.ds(i * COL_STEP, COL_STEP), pl.ds(src * ROWS_HERE, ROWS_HERE)]
        return pltpu.make_async_remote_copy(
            place, place, ci_s.at[i, d - 1], ci_r.at[i, d - 1],
            device_id=col_peer(d)[1], device_id_type=MESH,
        )

    def row_out_copy(i, part, d):
        other, device = row_peer(d)
        return pltpu.make_async_remote_copy(
            row_out.at[pl.ds(2 * part, 2), pl.ds(i * ROW_STEP, ROW_STEP), pl.ds(other * COLS_HERE, COLS_HERE)],
            raw_row.at[pl.ds(2 * part, 2), pl.ds(i * ROW_STEP, ROW_STEP), :, lanes(y)],
            ro_s.at[i, part, d - 1], ro_r.at[i, part, d - 1], device_id=device, device_id_type=MESH,
        )

    def row_out_own(i, part):
        return pltpu.make_async_copy(
            row_out.at[pl.ds(2 * part, 2), pl.ds(i * ROW_STEP, ROW_STEP), pl.ds(y * COLS_HERE, COLS_HERE)],
            raw_row.at[pl.ds(2 * part, 2), pl.ds(i * ROW_STEP, ROW_STEP), :, lanes(y)],
            ro_l.at[i, part],
        )

    def row_out_arrival(i, part, d):
        src = (y + 4 - d) % 4
        place = raw_row.at[pl.ds(2 * part, 2), pl.ds(i * ROW_STEP, ROW_STEP), :, lanes(src)]
        return pltpu.make_async_remote_copy(
            place, place, ro_s.at[i, part, d - 1], ro_r.at[i, part, d - 1],
            device_id=row_peer(d)[1], device_id_type=MESH,
        )

    def col_out_copy(i, part, d):
        other, device = col_peer(d)
        return pltpu.make_async_remote_copy(
            col_out.at[pl.ds(2 * part, 2), pl.ds(i * COL_STEP, COL_STEP), pl.ds(other * ROWS_HERE, ROWS_HERE)],
            raw_col.at[pl.ds(2 * part, 2), pl.ds(core * COL_BLOCK + i * COL_STEP, COL_STEP), :, lanes(x)],
            co_s.at[i, part, d - 1], co_r.at[i, part, d - 1], device_id=device, device_id_type=MESH,
        )

    def col_out_own(i, part):
        return pltpu.make_async_copy(
            col_out.at[pl.ds(2 * part, 2), pl.ds(i * COL_STEP, COL_STEP), pl.ds(xc * ROWS_HERE, ROWS_HERE)],
            raw_col.at[pl.ds(2 * part, 2), pl.ds(core * COL_BLOCK + i * COL_STEP, COL_STEP), :, lanes(x)],
            co_l.at[i, part],
        )

    def col_out_arrival(i, part, d):
        src = (xc + 8 - d) % 8
        place = raw_col.at[
            pl.ds(2 * part, 2), pl.ds((src % 2) * COL_BLOCK + i * COL_STEP, COL_STEP), :, lanes(src // 2)
        ]
        return pltpu.make_async_remote_copy(
            place, place, co_s.at[i, part, d - 1], co_r.at[i, part, d - 1],
            device_id=col_peer(d)[1], device_id_type=MESH,
        )

    def half_copy(i, upper, source, low, step, partner, s_sem, r_sem):
        return pltpu.make_async_remote_copy(
            source.at[pl.ds(0 if upper else 1, 2), pl.ds(i * step, step)],
            low.at[:, pl.ds(i * step, step)],
            s_sem.at[i], r_sem.at[i], device_id=partner, device_id_type=MESH,
        )

    row_half = functools.partial(half_copy, low=row_low, step=ROW_STEP, partner=row_partner, s_sem=rf_s, r_sem=rf_r)
    col_half = functools.partial(half_copy, low=col_low, step=COL_STEP, partner=col_partner, s_sem=cf_s, r_sem=cf_r)

    def issue_row(i, carry):
        for a in (1, 2, 0, 3):
            for d in (2, 1, 3):
                row_in_copy(i, a, d).start()
            row_in_own(i, a).start()
        return carry

    issue_row(0, 0)

    to = lax.broadcasted_iota(jnp.int32, (256, 256), 0)
    frm = lax.broadcasted_iota(jnp.int32, (256, 256), 1)
    turn = jnp.where(frm == (to % 16) * 16 + to // 16, 1.0, 0.0).astype(jnp.bfloat16)

    def turn_blocks(part):
        def one(t, carry):
            a, at = t // 2, (t % 2) * COL_BLOCK + part * 16
            block = stage[a, :, pl.ds(pl.multiple_of(at, 16), 16), :].reshape(256, HALF)
            turned = dot(turn, block, NN).astype(jnp.bfloat16).reshape(16, 16, HALF)
            send[a, pl.ds(at, 16)] = turned
            return carry

        lax.fori_loop(0, 8, one, 0)
        for j in range(STEPS // 2):
            i = part * (STEPS // 2) + j
            for d in (4, 5, 2, 3, 6, 7, 1):
                col_in_copy(i, d).start()
            col_in_own(i).start()

    for a in range(4):
        pltpu.make_async_copy(inputs[a].at[:, :, pl.ds(HALF, HALF)], stage.at[a], st_l.at[a]).wait()
    turn_blocks(0)
    lax.fori_loop(1, STEPS // 2, issue_row, 0)
    turn_blocks(1)
    lax.fori_loop(STEPS // 2, STEPS, issue_row, 0)

    def send_row(i, part):
        for d in (2, 1, 3):
            row_out_copy(i, part, d).start()
        row_out_own(i, part).start()

    def send_col(i, part):
        for d in (4, 5, 2, 3, 6, 7, 1):
            col_out_copy(i, part, d).start()
        col_out_own(i, part).start()

    def work(upper, box, low, out, part, keep, step, i):
        def one(n, carry):
            q, k, v, g = [box[a, n] for a in range(4)]
            if upper:
                found = attend(q, k, v, g, low[0, n], low[1, n])
                for a in range(4):
                    out[a, n] = found[a].astype(jnp.bfloat16)
                part[0, n] = found[4].astype(jnp.bfloat16)
                part[1, n] = found[5].astype(jnp.bfloat16)
            else:
                found = attend(q, k, v, g, None, None)
                out[0, n] = found[0].astype(jnp.bfloat16)
                out[1, n] = found[1].astype(jnp.bfloat16)
                keep[0, n] = found[2]
                keep[1, n] = found[3]
            return carry

        lax.fori_loop(i * step, (i + 1) * step, one, 0)

    def finish(half, low, out, keep, step, i):
        half(i, True, low).wait_recv()

        def one(n, carry):
            for a in range(2):
                out[2 + a, n] = (keep[a, n] + low[a, n].astype(jnp.float32)).astype(jnp.bfloat16)
            return carry

        lax.fori_loop(i * step, (i + 1) * step, one, 0)

    def row_step(i):
        for a in (1, 2, 0, 3):
            for d in range(1, 4):
                row_in_arrival(i, a, d).wait_recv()
            row_in_own(i, a).wait()

        @pl.when(z_hi == 0)
        def _():
            row_half(i, False, row_in).start()
            work(False, row_in, row_low, row_out, row_part, row_keep, ROW_STEP, i)
            send_row(i, 0)

        @pl.when(z_hi == 1)
        def _():
            row_half(i, True, row_part).wait_recv()
            work(True, row_in, row_low, row_out, row_part, row_keep, ROW_STEP, i)
            row_half(i, True, row_part).start()
            send_row(i, 0)
            send_row(i, 1)

    def col_step(i):
        for d in range(1, 8):
            col_in_arrival(i, d).wait_recv()
        col_in_own(i).wait()

        @pl.when(z_lo == 0)
        def _():
            col_half(i, False, col_in).start()
            work(False, col_in, col_low, col_out, col_part, col_keep, COL_STEP, i)
            send_col(i, 0)

        @pl.when(z_lo == 1)
        def _():
            col_half(i, True, col_part).wait_recv()
            work(True, col_in, col_low, col_out, col_part, col_keep, COL_STEP, i)
            col_half(i, True, col_part).start()
            send_col(i, 0)
            send_col(i, 1)

    def row_finish(i):
        @pl.when(z_hi == 0)
        def _():
            finish(row_half, row_low, row_out, row_keep, ROW_STEP, i)
            send_row(i, 1)

    def col_finish(i):
        @pl.when(z_lo == 0)
        def _():
            finish(col_half, col_low, col_out, col_keep, COL_STEP, i)
            send_col(i, 1)

    def step(i, carry):
        row_step(i)
        col_step(i)

        @pl.when(i > 0)
        def _():
            row_finish(i - 1)
            col_finish(i - 1)

        return carry

    lax.fori_loop(0, STEPS, step, 0)
    row_finish(STEPS - 1)
    col_finish(STEPS - 1)

    def drain(i, carry):
        for a in range(4):
            for d in range(1, 4):
                row_in_copy(i, a, d).wait_send()
        for d in range(1, 8):
            col_in_copy(i, d).wait_send()
        for part in range(2):
            for d in range(1, 4):
                row_out_copy(i, part, d).wait_send()
            for d in range(1, 8):
                col_out_copy(i, part, d).wait_send()
        row_half(i, True, row_part).wait_send()
        col_half(i, True, col_part).wait_send()
        for part in range(2):
            row_out_own(i, part).wait()
            col_out_own(i, part).wait()
            for d in range(1, 4):
                row_out_arrival(i, part, d).wait_recv()
            for d in range(1, 8):
                col_out_arrival(i, part, d).wait_recv()
        return carry

    lax.fori_loop(0, STEPS, drain, 0)


def exchange(queries, keys, values, grad_output):
    bf16, f32 = jnp.bfloat16, jnp.float32
    dma = pltpu.SemaphoreType.DMA

    def side(many, length):
        return [
            pltpu.VMEM((4, many, length, LANES), bf16),
            pltpu.VMEM((2, many, length, LANES), bf16),
            pltpu.VMEM((4, many, length, LANES), bf16),
            pltpu.VMEM((2, many, length, LANES), bf16),
            pltpu.VMEM((2, many, length, LANES), f32),
        ]

    return pl.pallas_call(
        body,
        out_shape=[
            jax.ShapeDtypeStruct((4, ROWS_HERE, COLS_HERE, HALF), bf16),
            jax.ShapeDtypeStruct((4, COLS_HERE, ROWS_HERE, HALF), bf16),
        ],
        in_specs=[pl.BlockSpec(memory_space=pl.ANY)] * 4,
        out_specs=[pl.BlockSpec(memory_space=pl.ANY)] * 2,
        scratch_shapes=side(ROWS_HERE, ROW_SEQ)
        + side(COL_BLOCK, COL_SEQ)
        + [pltpu.VMEM((4, ROWS_HERE, COLS_HERE, HALF), bf16), pltpu.VMEM((4, COLS_HERE, ROWS_HERE, HALF), bf16)]
        + [dma((STEPS, 4, 3)), dma((STEPS, 4, 3)), dma((STEPS, 4))]
        + [dma((STEPS, 7)), dma((STEPS, 7)), dma((STEPS,))]
        + [dma((STEPS, 2, 3)), dma((STEPS, 2, 3)), dma((STEPS, 2))]
        + [dma((STEPS, 2, 7)), dma((STEPS, 2, 7)), dma((STEPS, 2))]
        + [dma((STEPS,))] * 4
        + [dma((4,))],
        compiler_params=pltpu.CompilerParams(
            collective_id=0, has_side_effects=True, vmem_limit_bytes=60 * 2**20
        ),
        name="exchange",
    )(queries, keys, values, grad_output)


def join_body(row_ref, col_ref, *outs):
    to = lax.broadcasted_iota(jnp.int32, (256, 256), 0)
    frm = lax.broadcasted_iota(jnp.int32, (256, 256), 1)
    turn = jnp.where(frm == (to % 16) * 16 + to // 16, 1.0, 0.0).astype(jnp.bfloat16)
    for a in range(4):
        outs[a][:, :, :HALF] = row_ref[a]
        turned = dot(turn, col_ref[a].reshape(256, HALF), NN)
        outs[a][:, :, HALF:] = turned.astype(jnp.bfloat16).reshape(16, 16, HALF)


def join(raw_row, raw_col):
    shape = jax.ShapeDtypeStruct((ROWS_HERE, COLS_HERE, 2 * HALF), jnp.bfloat16)
    return pl.pallas_call(
        join_body,
        grid=(COLS_HERE // 16,),
        out_shape=[shape] * 4,
        in_specs=[
            pl.BlockSpec((4, ROWS_HERE, 16, HALF), lambda i: (0, 0, i, 0)),
            pl.BlockSpec((4, 16, ROWS_HERE, HALF), lambda i: (0, i, 0, 0)),
        ],
        out_specs=[pl.BlockSpec((ROWS_HERE, 16, 2 * HALF), lambda i: (0, i, 0))] * 4,
        compiler_params=pltpu.CompilerParams(vmem_limit_bytes=48 * 2**20),
        name="join",
    )(raw_row, raw_col)


def on_device(queries, keys, values, grad_output):
    raw_row, raw_col = exchange(queries, keys, values, grad_output)
    return tuple(join(raw_row, raw_col))


def solution(mesh):
    spec = P("row", "col", None)
    return jax.shard_map(
        on_device, mesh=mesh, in_specs=(spec,) * 4, out_specs=(spec,) * 4, check_vma=False
    )
```

```python
import functools

import jax
import jax.numpy as jnp
from jax import lax
from jax.experimental import pallas as pl
from jax.experimental.pallas import tpu as pltpu
from jax.sharding import PartitionSpec as P

MESH = pl.DeviceIdType.MESH
STEPS = 8
LAG = 3
LANES = 128
HALF = 512
ROWS_HERE = 16
COLS_HERE = 64
ROW_SEQ = 256
COL_SEQ = 128
COL_BLOCK = 32
ROW_STEP = ROWS_HERE // STEPS
COL_STEP = COL_BLOCK // STEPS
ROW_UNROLL = min(ROW_STEP, 2)
COL_UNROLL = min(COL_STEP, 4)
NT = (((1,), (1,)), ((), ()))
TN = (((0,), (0,)), ((), ()))
NN = (((1,), (0,)), ((), ()))


def dot(a, b, dims):
    return lax.dot_general(a, b, dims, preferred_element_type=jnp.float32)


def attend(q, k, v, g, k_low, v_low):
    length = q.shape[0]
    keys_at = lax.broadcasted_iota(jnp.int32, (length, 2 * length), 0)
    queries_at = lax.broadcasted_iota(jnp.int32, (length, 2 * length), 1) % length
    allowed = keys_at <= queries_at
    parts = [(k, v)] if k_low is None else [(k, v), (k_low, v_low)]
    q_t = (q * jnp.bfloat16(0.125)).T
    g_t = g.T
    flipped = [(pk.T, pv.T) for pk, pv in parts]
    blank = jnp.zeros((64, length), jnp.bfloat16)
    heads = (slice(0, 64), slice(64, 128))
    cols = (slice(0, length), slice(length, 2 * length))

    def beside(first, second):
        return jnp.concatenate(
            [jnp.concatenate([first, blank], axis=0), jnp.concatenate([blank, second], axis=0)], axis=1
        )

    def per_head(lefts, rights, extra):
        found = []
        if length <= 128:
            both = 0.0
            for left, right in zip(lefts, rights):
                rows = left
                if extra:
                    rows = jnp.concatenate([left, jnp.ones((16, left.shape[1]), jnp.bfloat16)], axis=0)
                both = both + dot(rows, right, NN)
            for rows, at in zip(heads, cols):
                found.append((both[rows, at], both[128:129, at] if extra else None))
            return found
        for rows, at in zip(heads, cols):
            one = 0.0
            for left, right in zip(lefts, rights):
                mine = left[rows]
                if extra:
                    mine = jnp.concatenate([mine, jnp.ones((16, left.shape[1]), jnp.bfloat16)], axis=0)
                one = one + dot(mine, right[:, at], NN)
            found.append((one[:64], one[64:65] if extra else None))
        return found

    q_both, g_both = beside(q_t[:64], q_t[64:]), beside(g_t[:64], g_t[64:])
    scores = [dot(pk, q_both, NN) for pk, _ in parts]
    dprobs = [dot(pv, g_both, NN) for _, pv in parts]
    scores[0] = jnp.where(allowed, scores[0], -1e30)
    top = functools.reduce(jnp.maximum, [jnp.max(s, axis=0, keepdims=True) for s in scores])
    weights = [jnp.exp(s - top) for s in scores]
    low = [w.astype(jnp.bfloat16) for w in weights]
    summed = per_head([v_t for _, v_t in flipped], low, True)
    inverse = [1.0 / norm for _, norm in summed]
    attended = [total * inv for (total, _), inv in zip(summed, inverse)]
    g_here = [g_t[rows].astype(jnp.float32) for rows in heads]
    delta = jnp.concatenate(
        [jnp.sum(a * b, axis=0, keepdims=True) for a, b in zip(g_here, attended)], axis=1
    )
    ds = [(w * (d - delta)).astype(jnp.bfloat16) for w, d in zip(weights, dprobs)]
    dq = per_head([k_t for k_t, _ in flipped], ds, False)
    dq = [total * (inv * 0.125) for (total, _), inv in zip(dq, inverse)]
    q_scaled = beside(*[(q_t[r].astype(jnp.float32) * inv).astype(jnp.bfloat16) for r, inv in zip(heads, inverse)])
    g_scaled = beside(*[(gh * inv).astype(jnp.bfloat16) for gh, inv in zip(g_here, inverse)])
    found = [jnp.concatenate([t.astype(jnp.bfloat16) for t in two], axis=0).T for two in (attended, dq)]
    for d, w in zip(ds, low):
        found += [dot(d, q_scaled, NT), dot(w, g_scaled, NT)]
    return found


def body(
    q_ref, k_ref, v_ref, g_ref, raw_row, raw_col,
    row_in, row_low, row_out, row_part, row_keep,
    col_in, col_low, col_out, col_part, col_keep,
    stage, send,
    ri_s, ri_r, ri_l, ci_s, ci_r, ci_l,
    ro_s, ro_r, ro_l, co_s, co_r, co_l,
    rf_s, rf_r, cf_s, cf_r, st_l,
):
    inputs = (q_ref, k_ref, v_ref, g_ref)
    row, col = lax.axis_index("row"), lax.axis_index("col")
    z_lo, xc = row // 8, row % 8
    x, core = xc // 2, xc % 2
    z_hi, y = col // 4, col % 4

    def row_peer(d):
        other = (y + d) % 4
        return other, (row, z_hi * 4 + other)

    def col_peer(d):
        other = (xc + d) % 8
        return other, (z_lo * 8 + other, col)

    row_partner = (row, (1 - z_hi) * 4 + y)
    col_partner = ((1 - z_lo) * 8 + xc, col)

    def stage_copy(a, part, core_of):
        at = pl.ds(core_of * COL_BLOCK + part * 16, 16)
        return pltpu.make_async_copy(
            inputs[a].at[:, at, pl.ds(HALF, HALF)], stage.at[a, :, at], st_l.at[a, part, core_of]
        )

    for part in range(2):
        for a in range(4):
            for core_of in range(2):
                stage_copy(a, part, core_of).start()

    barrier = pltpu.get_barrier_semaphore()
    everyone = [row_peer(d)[1] for d in range(1, 4)] + [col_peer(d)[1] for d in range(1, 8)]
    everyone += [row_partner, col_partner]
    for device in everyone:
        pl.semaphore_signal(barrier, inc=1, device_id=device, device_id_type=MESH)

    def lanes(i):
        return pl.ds(pl.multiple_of(i * LANES, LANES), LANES)

    def row_in_copy(i, a, d):
        other, device = row_peer(d)
        return pltpu.make_async_remote_copy(
            inputs[a].at[pl.ds(i * ROW_STEP, ROW_STEP), :, lanes(other)],
            row_in.at[a, pl.ds(i * ROW_STEP, ROW_STEP), pl.ds(y * COLS_HERE, COLS_HERE)],
            ri_s.at[i, a, d - 1], ri_r.at[i, a, d - 1], device_id=device, device_id_type=MESH,
        )

    def row_in_own(i, a):
        return pltpu.make_async_copy(
            inputs[a].at[pl.ds(i * ROW_STEP, ROW_STEP), :, lanes(y)],
            row_in.at[a, pl.ds(i * ROW_STEP, ROW_STEP), pl.ds(y * COLS_HERE, COLS_HERE)],
            ri_l.at[i, a],
        )

    def row_in_arrival(i, a, d):
        src = (y + 4 - d) % 4
        place = row_in.at[a, pl.ds(i * ROW_STEP, ROW_STEP), pl.ds(src * COLS_HERE, COLS_HERE)]
        return pltpu.make_async_remote_copy(
            place, place, ri_s.at[i, a, d - 1], ri_r.at[i, a, d - 1],
            device_id=row_peer(d)[1], device_id_type=MESH,
        )

    def col_in_copy(i, d):
        other, device = col_peer(d)
        return pltpu.make_async_remote_copy(
            send.at[:, pl.ds((other % 2) * COL_BLOCK + i * COL_STEP, COL_STEP), :, lanes(other // 2)],
            col_in.at[:, pl.ds(i * COL_STEP, COL_STEP), pl.ds(xc * ROWS_HERE, ROWS_HERE)],
            ci_s.at[i, d - 1], ci_r.at[i, d - 1], device_id=device, device_id_type=MESH,
        )

    def col_in_own(i):
        return pltpu.make_async_copy(
            send.at[:, pl.ds(core * COL_BLOCK + i * COL_STEP, COL_STEP), :, lanes(x)],
            col_in.at[:, pl.ds(i * COL_STEP, COL_STEP), pl.ds(xc * ROWS_HERE, ROWS_HERE)],
            ci_l.at[i],
        )

    def col_in_arrival(i, d):
        src = (xc + 8 - d) % 8
        place = col_in.at[:, pl.ds(i * COL_STEP, COL_STEP), pl.ds(src * ROWS_HERE, ROWS_HERE)]
        return pltpu.make_async_remote_copy(
            place, place, ci_s.at[i, d - 1], ci_r.at[i, d - 1],
            device_id=col_peer(d)[1], device_id_type=MESH,
        )

    def which(part):
        return pl.ds(0, 4) if part == 2 else pl.ds(2 * part, 2)

    def row_out_copy(i, part, d):
        other, device = row_peer(d)
        return pltpu.make_async_remote_copy(
            row_out.at[which(part), pl.ds(i * ROW_STEP, ROW_STEP), pl.ds(other * COLS_HERE, COLS_HERE)],
            raw_row.at[which(part), pl.ds(i * ROW_STEP, ROW_STEP), :, lanes(y)],
            ro_s.at[i, part % 2, d - 1], ro_r.at[i, part % 2, d - 1], device_id=device, device_id_type=MESH,
        )

    def row_out_own(i, part):
        return pltpu.make_async_copy(
            row_out.at[which(part), pl.ds(i * ROW_STEP, ROW_STEP), pl.ds(y * COLS_HERE, COLS_HERE)],
            raw_row.at[which(part), pl.ds(i * ROW_STEP, ROW_STEP), :, lanes(y)],
            ro_l.at[i, part % 2],
        )

    def row_out_arrival(i, part, d):
        src = (y + 4 - d) % 4
        place = raw_row.at[which(part), pl.ds(i * ROW_STEP, ROW_STEP), :, lanes(src)]
        return pltpu.make_async_remote_copy(
            place, place, ro_s.at[i, part % 2, d - 1], ro_r.at[i, part % 2, d - 1],
            device_id=row_peer(d)[1], device_id_type=MESH,
        )

    def col_out_copy(i, part, d):
        other, device = col_peer(d)
        return pltpu.make_async_remote_copy(
            col_out.at[which(part), pl.ds(i * COL_STEP, COL_STEP), pl.ds(other * ROWS_HERE, ROWS_HERE)],
            raw_col.at[which(part), pl.ds(core * COL_BLOCK + i * COL_STEP, COL_STEP), :, lanes(x)],
            co_s.at[i, part % 2, d - 1], co_r.at[i, part % 2, d - 1], device_id=device, device_id_type=MESH,
        )

    def col_out_own(i, part):
        return pltpu.make_async_copy(
            col_out.at[which(part), pl.ds(i * COL_STEP, COL_STEP), pl.ds(xc * ROWS_HERE, ROWS_HERE)],
            raw_col.at[which(part), pl.ds(core * COL_BLOCK + i * COL_STEP, COL_STEP), :, lanes(x)],
            co_l.at[i, part % 2],
        )

    def col_out_arrival(i, part, d):
        src = (xc + 8 - d) % 8
        place = raw_col.at[
            which(part), pl.ds((src % 2) * COL_BLOCK + i * COL_STEP, COL_STEP), :, lanes(src // 2)
        ]
        return pltpu.make_async_remote_copy(
            place, place, co_s.at[i, part % 2, d - 1], co_r.at[i, part % 2, d - 1],
            device_id=col_peer(d)[1], device_id_type=MESH,
        )

    def half_copy(i, upper, source, low, step, partner, s_sem, r_sem):
        return pltpu.make_async_remote_copy(
            source.at[pl.ds(0 if upper else 1, 2), pl.ds(i * step, step)],
            low.at[:, pl.ds(i * step, step)],
            s_sem.at[i], r_sem.at[i], device_id=partner, device_id_type=MESH,
        )

    row_half = functools.partial(half_copy, low=row_low, step=ROW_STEP, partner=row_partner, s_sem=rf_s, r_sem=rf_r)
    col_half = functools.partial(half_copy, low=col_low, step=COL_STEP, partner=col_partner, s_sem=cf_s, r_sem=cf_r)

    def issue_row(i, carry):
        for a in (1, 2, 0, 3):
            for d in (2, 1, 3):
                row_in_copy(i, a, d).start()
            row_in_own(i, a).start()
        return carry

    to = lax.broadcasted_iota(jnp.int32, (256, 256), 0)
    frm = lax.broadcasted_iota(jnp.int32, (256, 256), 1)
    turn = jnp.where(frm == (to % 16) * 16 + to // 16, 1.0, 0.0).astype(jnp.bfloat16)

    def turn_blocks(part):
        for a in range(4):
            for core_of in range(2):
                stage_copy(a, part, core_of).wait()

        def one(a, carry):
            for core_of in range(2):
                at = core_of * COL_BLOCK + part * 16
                block = stage[a, :, pl.ds(at, 16), :].reshape(256, HALF)
                turned = dot(turn, block, NN).astype(jnp.bfloat16).reshape(16, 16, HALF)
                send[a, pl.ds(at, 16)] = turned
            return carry

        lax.fori_loop(0, 4, one, 0)

    def issue_col(i, carry):
        for d in (4, 5, 2, 3, 6, 7, 1):
            col_in_copy(i, d).start()
        col_in_own(i).start()
        return carry

    turn_blocks(0)
    pl.semaphore_wait(barrier, len(everyone))
    issue_row(0, 0)
    lax.fori_loop(0, STEPS // 2, issue_col, 0)
    lax.fori_loop(1, STEPS // 2, issue_row, 0)
    turn_blocks(1)
    lax.fori_loop(STEPS // 2, STEPS, issue_col, 0)
    lax.fori_loop(STEPS // 2, STEPS, issue_row, 0)

    def send_row(i, part):
        for d in (2, 1, 3):
            row_out_copy(i, part, d).start()
        row_out_own(i, part).start()

    def send_col(i, part):
        for d in (4, 5, 2, 3, 6, 7, 1):
            col_out_copy(i, part, d).start()
        col_out_own(i, part).start()

    def work(upper, box, low, out, part, keep, step, unroll, i):
        def one(n):
            q, k, v, g = [box[a, n] for a in range(4)]
            if upper:
                found = attend(q, k, v, g, low[0, n], low[1, n])
                for a in range(4):
                    out[a, n] = found[a].astype(jnp.bfloat16)
                part[0, n] = found[4].astype(jnp.bfloat16)
                part[1, n] = found[5].astype(jnp.bfloat16)
            else:
                found = attend(q, k, v, g, None, None)
                out[0, n] = found[0].astype(jnp.bfloat16)
                out[1, n] = found[1].astype(jnp.bfloat16)
                keep[0, n] = found[2]
                keep[1, n] = found[3]

        def some(m, carry):
            for u in range(unroll):
                one(i * step + m * unroll + u)
            return carry

        lax.fori_loop(0, step // unroll, some, 0)

    def finish(half, low, out, keep, step, i):
        half(i, True, low).wait_recv()

        def one(n, carry):
            for a in range(2):
                out[2 + a, n] = (keep[a, n] + low[a, n].astype(jnp.float32)).astype(jnp.bfloat16)
            return carry

        lax.fori_loop(i * step, (i + 1) * step, one, 0)

    def arrive(i):
        for a in range(4):
            for d in range(1, 4):
                row_in_arrival(i, a, d).wait_recv()
            row_in_own(i, a).wait()

        @pl.when(z_hi == 0)
        def _():
            row_half(i, False, row_in).start()

        for d in range(1, 8):
            col_in_arrival(i, d).wait_recv()
        col_in_own(i).wait()

        @pl.when(z_lo == 0)
        def _():
            col_half(i, False, col_in).start()

    def lower_work(i):
        @pl.when(z_hi == 0)
        def _():
            work(False, row_in, row_low, row_out, row_part, row_keep, ROW_STEP, ROW_UNROLL, i)
            send_row(i, 0)

        @pl.when(z_lo == 0)
        def _():
            work(False, col_in, col_low, col_out, col_part, col_keep, COL_STEP, COL_UNROLL, i)
            send_col(i, 0)

    def upper_work(i):
        @pl.when(z_hi == 1)
        def _():
            row_half(i, True, row_part).wait_recv()
            work(True, row_in, row_low, row_out, row_part, row_keep, ROW_STEP, ROW_UNROLL, i)
            row_half(i, True, row_part).start()
            send_row(i, 2)

        @pl.when(z_lo == 1)
        def _():
            col_half(i, True, col_part).wait_recv()
            work(True, col_in, col_low, col_out, col_part, col_keep, COL_STEP, COL_UNROLL, i)
            col_half(i, True, col_part).start()
            send_col(i, 2)

    def finish_lower(i):
        @pl.when(z_hi == 0)
        def _():
            finish(row_half, row_low, row_out, row_keep, ROW_STEP, i)
            send_row(i, 1)

        @pl.when(z_lo == 0)
        def _():
            finish(col_half, col_low, col_out, col_keep, COL_STEP, i)
            send_col(i, 1)

    arrive(0)

    def step(i, carry):
        @pl.when(i < STEPS - 1)
        def _():
            arrive(i + 1)

        lower_work(i)
        upper_work(i)

        @pl.when(i >= LAG)
        def _():
            finish_lower(i - LAG)

        return carry

    lax.fori_loop(0, STEPS, step, 0)

    def late(i, carry):
        finish_lower(i)
        return carry

    lax.fori_loop(STEPS - LAG, STEPS, late, 0)

    def drain_out(i, upper, own, copy, arrival, count):
        @pl.when(upper)
        def _():
            own(i, 2).wait()
            for d in range(1, count):
                arrival(i, 2, d).wait_recv()
                copy(i, 2, d).wait_send()

        @pl.when(jnp.logical_not(upper))
        def _():
            for part in range(2):
                own(i, part).wait()
                for d in range(1, count):
                    arrival(i, part, d).wait_recv()
                    copy(i, part, d).wait_send()

    def drain(i, carry):
        for a in range(4):
            for d in range(1, 4):
                row_in_copy(i, a, d).wait_send()
        for d in range(1, 8):
            col_in_copy(i, d).wait_send()
        row_half(i, True, row_part).wait_send()
        col_half(i, True, col_part).wait_send()
        drain_out(i, z_hi == 1, row_out_own, row_out_copy, row_out_arrival, 4)
        drain_out(i, z_lo == 1, col_out_own, col_out_copy, col_out_arrival, 8)
        return carry

    lax.fori_loop(0, STEPS, drain, 0)


def exchange(queries, keys, values, grad_output):
    bf16, f32 = jnp.bfloat16, jnp.float32
    dma = pltpu.SemaphoreType.DMA

    def side(many, length):
        return [
            pltpu.VMEM((4, many, length, LANES), bf16),
            pltpu.VMEM((2, many, length, LANES), bf16),
            pltpu.VMEM((4, many, length, LANES), bf16),
            pltpu.VMEM((2, many, length, LANES), bf16),
            pltpu.VMEM((2, many, length, LANES), f32),
        ]

    return pl.pallas_call(
        body,
        out_shape=[
            jax.ShapeDtypeStruct((4, ROWS_HERE, COLS_HERE, HALF), bf16),
            jax.ShapeDtypeStruct((4, COLS_HERE, ROWS_HERE, HALF), bf16),
        ],
        in_specs=[pl.BlockSpec(memory_space=pl.ANY)] * 4,
        out_specs=[pl.BlockSpec(memory_space=pl.ANY)] * 2,
        scratch_shapes=side(ROWS_HERE, ROW_SEQ)
        + side(COL_BLOCK, COL_SEQ)
        + [pltpu.VMEM((4, ROWS_HERE, COLS_HERE, HALF), bf16), pltpu.VMEM((4, COLS_HERE, ROWS_HERE, HALF), bf16)]
        + [dma((STEPS, 4, 3)), dma((STEPS, 4, 3)), dma((STEPS, 4))]
        + [dma((STEPS, 7)), dma((STEPS, 7)), dma((STEPS,))]
        + [dma((STEPS, 2, 3)), dma((STEPS, 2, 3)), dma((STEPS, 2))]
        + [dma((STEPS, 2, 7)), dma((STEPS, 2, 7)), dma((STEPS, 2))]
        + [dma((STEPS,))] * 4
        + [dma((4, 2, 2))],
        compiler_params=pltpu.CompilerParams(
            collective_id=0, has_side_effects=True, vmem_limit_bytes=60 * 2**20
        ),
        name="exchange",
    )(queries, keys, values, grad_output)


def join_body(row_ref, col_ref, *outs):
    to = lax.broadcasted_iota(jnp.int32, (256, 256), 0)
    frm = lax.broadcasted_iota(jnp.int32, (256, 256), 1)
    turn = jnp.where(frm == (to % 16) * 16 + to // 16, 1.0, 0.0).astype(jnp.bfloat16)
    for a in range(4):
        outs[a][:, :, :HALF] = row_ref[a]
        turned = dot(turn, col_ref[a].reshape(256, HALF), NN)
        outs[a][:, :, HALF:] = turned.astype(jnp.bfloat16).reshape(16, 16, HALF)


def join(raw_row, raw_col):
    shape = jax.ShapeDtypeStruct((ROWS_HERE, COLS_HERE, 2 * HALF), jnp.bfloat16)
    return pl.pallas_call(
        join_body,
        grid=(COLS_HERE // 16,),
        out_shape=[shape] * 4,
        in_specs=[
            pl.BlockSpec((4, ROWS_HERE, 16, HALF), lambda i: (0, 0, i, 0)),
            pl.BlockSpec((4, 16, ROWS_HERE, HALF), lambda i: (0, i, 0, 0)),
        ],
        out_specs=[pl.BlockSpec((ROWS_HERE, 16, 2 * HALF), lambda i: (0, i, 0))] * 4,
        compiler_params=pltpu.CompilerParams(vmem_limit_bytes=48 * 2**20),
        name="join",
    )(raw_row, raw_col)


def on_device(queries, keys, values, grad_output):
    raw_row, raw_col = exchange(queries, keys, values, grad_output)
    return tuple(join(raw_row, raw_col))


def solution(mesh):
    spec = P("row", "col", None)
    return jax.shard_map(
        on_device, mesh=mesh, in_specs=(spec,) * 4, out_specs=(spec,) * 4, check_vma=False
    )
```

```python
import functools

import jax
import jax.numpy as jnp
from jax import lax
from jax.experimental import pallas as pl
from jax.experimental.pallas import tpu as pltpu
from jax.sharding import PartitionSpec as P

MESH = pl.DeviceIdType.MESH
STEPS = 16
LAG = 5
LANES = 128
HALF = 512
ROWS_HERE = 16
COLS_HERE = 64
ROW_SEQ = 256
COL_SEQ = 128
COL_BLOCK = 32
ROW_STEP = ROWS_HERE // STEPS
COL_STEP = COL_BLOCK // STEPS
ROW_UNROLL = min(ROW_STEP, 2)
COL_UNROLL = min(COL_STEP, 4)
NT = (((1,), (1,)), ((), ()))
NN = (((1,), (0,)), ((), ()))


def dot(a, b, dims):
    return lax.dot_general(a, b, dims, preferred_element_type=jnp.float32)


def beside(first, second):
    blank = jnp.zeros_like(first)
    return jnp.concatenate(
        [jnp.concatenate([first, blank], axis=0), jnp.concatenate([blank, second], axis=0)], axis=1
    )


def per_head(lefts, rights, norms):
    length = rights[0].shape[1] // 2
    heads = (slice(0, 64), slice(64, 128))
    cols = (slice(0, length), slice(length, 2 * length))

    def with_ones(rows):
        if not norms:
            return rows
        return jnp.concatenate([rows, jnp.ones((16, rows.shape[1]), jnp.bfloat16)], axis=0)

    if length <= 128:
        both = sum(dot(with_ones(left), right, NN) for left, right in zip(lefts, rights))
        return [(both[rows, at], both[128:129, at] if norms else None) for rows, at in zip(heads, cols)]
    found = []
    for rows, at in zip(heads, cols):
        one = sum(dot(with_ones(left[rows]), right[:, at], NN) for left, right in zip(lefts, rights))
        found.append((one[:64], one[64:65] if norms else None))
    return found


def over_queries(two):
    return jnp.concatenate(two, axis=1)


def natural(two):
    return jnp.concatenate([t.astype(jnp.bfloat16) for t in two], axis=0).T


def split(pair):
    return pair[:64], pair[64:]


def attend(q, k, v, g, k_low=None, v_low=None):
    length = q.shape[0]
    keys_at = lax.broadcasted_iota(jnp.int32, (length, 2 * length), 0)
    queries_at = lax.broadcasted_iota(jnp.int32, (length, 2 * length), 1) % length
    parts = [(k, v)] if k_low is None else [(k, v), (k_low, v_low)]
    q_t = split((q * jnp.bfloat16(0.125)).T)
    g_t = split(g.T)
    flipped = [(pk.T, pv.T) for pk, pv in parts]
    q_both, g_both = beside(*q_t), beside(*g_t)
    scores = [dot(pk, q_both, NN) for pk, _ in parts]
    dprobs = [dot(pv, g_both, NN) for _, pv in parts]
    scores[0] = jnp.where(keys_at <= queries_at, scores[0], -1e30)
    top = functools.reduce(jnp.maximum, [jnp.max(s, axis=0, keepdims=True) for s in scores])
    weights = [jnp.exp(s - top) for s in scores]
    low = [w.astype(jnp.bfloat16) for w in weights]
    summed = per_head([v_t for _, v_t in flipped], low, True)
    norm = over_queries([n for _, n in summed])
    total = [t for t, _ in summed]
    scale = 1.0 / norm
    inverse = (scale[:, :length], scale[:, length:])
    attended = [t * inv for t, inv in zip(total, inverse)]
    g_here = [one.astype(jnp.float32) for one in g_t]
    delta = over_queries([jnp.sum(a * b, axis=0, keepdims=True) for a, b in zip(g_here, attended)])
    ds = [(w * (d - delta)).astype(jnp.bfloat16) for w, d in zip(weights, dprobs)]
    dq = [t * (inv * 0.125) for (t, _), inv in zip(per_head([k_t for k_t, _ in flipped], ds, False), inverse)]
    q_scaled = beside(*[(t.astype(jnp.float32) * inv).astype(jnp.bfloat16) for t, inv in zip(q_t, inverse)])
    g_scaled = beside(*[(t * inv).astype(jnp.bfloat16) for t, inv in zip(g_here, inverse)])
    found = [natural(attended), natural(dq)]
    for d, w in zip(ds, low):
        found += [dot(d, q_scaled, NT), dot(w, g_scaled, NT)]
    return found


def body(
    q_ref, k_ref, v_ref, g_ref, raw_row, raw_col,
    row_in, row_low, row_out, row_part, row_keep,
    col_in, col_low, col_out, col_part, col_keep,
    stage, send,
    ri_s, ri_r, ci_s, ci_r, ro_s, ro_r, co_s, co_r, rf_s, rf_r, cf_s, cf_r, st_l,
):
    inputs = (k_ref, v_ref, q_ref, g_ref)
    row, col = lax.axis_index("row"), lax.axis_index("col")
    z_lo, xc = row // 8, row % 8
    x, core = xc // 2, xc % 2
    z_hi, y = col // 4, col % 4

    def row_peer(d):
        other = (y + d) % 4
        return other, (row, z_hi * 4 + other)

    def col_peer(d):
        other = (xc + d) % 8
        return other, (z_lo * 8 + other, col)

    row_partner = (row, (1 - z_hi) * 4 + y)
    col_partner = ((1 - z_lo) * 8 + xc, col)

    def stage_copy(a, part, core_of):
        at = pl.ds(core_of * COL_BLOCK + part * 16, 16)
        return pltpu.make_async_copy(
            inputs[a].at[:, at, pl.ds(HALF, HALF)], stage.at[a, :, at], st_l.at[a, part, core_of]
        )

    for part in range(2):
        for a in range(4):
            for core_of in range(2):
                stage_copy(a, part, core_of).start()

    barrier = pltpu.get_barrier_semaphore()
    everyone = [row_peer(d)[1] for d in range(1, 4)] + [col_peer(d)[1] for d in range(1, 8)]
    everyone += [row_partner, col_partner]
    for device in everyone:
        pl.semaphore_signal(barrier, inc=1, device_id=device, device_id_type=MESH)

    def lanes(i):
        return pl.ds(pl.multiple_of(i * LANES, LANES), LANES)

    def row_in_copy(i, a, d):
        other, device = row_peer(d)
        return pltpu.make_async_remote_copy(
            inputs[a].at[pl.ds(i * ROW_STEP, ROW_STEP), :, lanes(other)],
            row_in.at[a, pl.ds(i * ROW_STEP, ROW_STEP), pl.ds(y * COLS_HERE, COLS_HERE)],
            ri_s.at[0], ri_r.at[i, a // 2], device_id=device, device_id_type=MESH,
        )

    def row_in_own(i, a):
        return pltpu.make_async_copy(
            inputs[a].at[pl.ds(i * ROW_STEP, ROW_STEP), :, lanes(y)],
            row_in.at[a, pl.ds(i * ROW_STEP, ROW_STEP), pl.ds(y * COLS_HERE, COLS_HERE)],
            ri_r.at[i, a // 2],
        )

    def col_in_copy(i, pair, d):
        other, device = col_peer(d)
        return pltpu.make_async_remote_copy(
            send.at[pl.ds(2 * pair, 2), pl.ds((other % 2) * COL_BLOCK + i * COL_STEP, COL_STEP), :, lanes(other // 2)],
            col_in.at[pl.ds(2 * pair, 2), pl.ds(i * COL_STEP, COL_STEP), pl.ds(xc * ROWS_HERE, ROWS_HERE)],
            ci_s.at[0], ci_r.at[i, pair], device_id=device, device_id_type=MESH,
        )

    def col_in_own(i, pair):
        return pltpu.make_async_copy(
            send.at[pl.ds(2 * pair, 2), pl.ds(core * COL_BLOCK + i * COL_STEP, COL_STEP), :, lanes(x)],
            col_in.at[pl.ds(2 * pair, 2), pl.ds(i * COL_STEP, COL_STEP), pl.ds(xc * ROWS_HERE, ROWS_HERE)],
            ci_r.at[i, pair],
        )

    def which(part):
        return pl.ds(0, 4) if part == 2 else pl.ds(2 * part, 2)

    def row_out_copy(i, part, d):
        other, device = row_peer(d)
        return pltpu.make_async_remote_copy(
            row_out.at[which(part), pl.ds(i * ROW_STEP, ROW_STEP), pl.ds(other * COLS_HERE, COLS_HERE)],
            raw_row.at[which(part), pl.ds(i * ROW_STEP, ROW_STEP), :, lanes(y)],
            ro_s.at[0], ro_r.at[0], device_id=device, device_id_type=MESH,
        )

    def row_out_own(i, part):
        return pltpu.make_async_copy(
            row_out.at[which(part), pl.ds(i * ROW_STEP, ROW_STEP), pl.ds(y * COLS_HERE, COLS_HERE)],
            raw_row.at[which(part), pl.ds(i * ROW_STEP, ROW_STEP), :, lanes(y)],
            ro_r.at[0],
        )

    def col_out_copy(i, part, d):
        other, device = col_peer(d)
        return pltpu.make_async_remote_copy(
            col_out.at[which(part), pl.ds(i * COL_STEP, COL_STEP), pl.ds(other * ROWS_HERE, ROWS_HERE)],
            raw_col.at[which(part), pl.ds(core * COL_BLOCK + i * COL_STEP, COL_STEP), :, lanes(x)],
            co_s.at[0], co_r.at[0], device_id=device, device_id_type=MESH,
        )

    def col_out_own(i, part):
        return pltpu.make_async_copy(
            col_out.at[which(part), pl.ds(i * COL_STEP, COL_STEP), pl.ds(xc * ROWS_HERE, ROWS_HERE)],
            raw_col.at[which(part), pl.ds(core * COL_BLOCK + i * COL_STEP, COL_STEP), :, lanes(x)],
            co_r.at[0],
        )

    class Side:
        pass

    def make_side(**fields):
        side = Side()
        for name, value in fields.items():
            setattr(side, name, value)
        return side

    def pair_copy(side, i, source):
        return pltpu.make_async_remote_copy(
            source.at[pl.ds(0, 2), pl.ds(i * side.step, side.step)],
            side.low.at[:, pl.ds(i * side.step, side.step)],
            side.f_s.at[0], side.f_r.at[i], device_id=side.partner, device_id_type=MESH,
        )

    def issue_row(i, pair):
        for a in (2 * pair, 2 * pair + 1):
            for d in (2, 1, 3):
                row_in_copy(i, a, d).start()
            row_in_own(i, a).start()

    to = lax.broadcasted_iota(jnp.int32, (256, 256), 0)
    frm = lax.broadcasted_iota(jnp.int32, (256, 256), 1)
    turn = jnp.where(frm == (to % 16) * 16 + to // 16, 1.0, 0.0).astype(jnp.bfloat16)

    def turn_blocks(part, pair):
        for a in (2 * pair, 2 * pair + 1):
            for core_of in range(2):
                stage_copy(a, part, core_of).wait()
                at = core_of * COL_BLOCK + part * 16
                block = stage[a, :, pl.ds(at, 16), :].reshape(256, HALF)
                turned = dot(turn, block, NN).astype(jnp.bfloat16).reshape(16, 16, HALF)
                send[a, pl.ds(at, 16)] = turned

    def issue_col(i, pair):
        for d in (4, 5, 2, 3, 6, 7, 1):
            col_in_copy(i, pair, d).start()
        col_in_own(i, pair).start()

    def issue(i, carry):
        for pair in range(2):
            issue_row(i, pair)
            issue_col(i, pair)
        return carry

    def send_row(i, part):
        for d in (2, 1, 3):
            row_out_copy(i, part, d).start()
        row_out_own(i, part).start()

    def send_col(i, part):
        for d in (4, 5, 2, 3, 6, 7, 1):
            col_out_copy(i, part, d).start()
        col_out_own(i, part).start()

    row_side = make_side(
        upper=z_hi == 1, step=ROW_STEP, unroll=ROW_UNROLL, length=ROW_SEQ, partner=row_partner,
        box=row_in, low=row_low, out=row_out, part=row_part, keep=row_keep, f_s=rf_s, f_r=rf_r,
        send=send_row,
    )
    col_side = make_side(
        upper=z_lo == 1, step=COL_STEP, unroll=COL_UNROLL, length=COL_SEQ, partner=col_partner,
        box=col_in, low=col_low, out=col_out, part=col_part, keep=col_keep, f_s=cf_s, f_r=cf_r,
        send=send_col,
    )

    def each(side, i, one):
        def some(m, carry):
            for u in range(side.unroll):
                one(i * side.step + m * side.unroll + u)
            return carry

        lax.fori_loop(0, side.step // side.unroll, some, 0)

    def bf16(value):
        return value.astype(jnp.bfloat16)

    def begin(side, i):
        def lower_one(n):
            k, v, q, g = [side.box[a, n] for a in range(4)]
            found = attend(q, k, v, g)
            side.out[0, n] = found[0]
            side.out[1, n] = found[1]
            side.keep[0, n] = found[2]
            side.keep[1, n] = found[3]

        def upper_one(n):
            k, v, q, g = [side.box[a, n] for a in range(4)]
            found = attend(q, k, v, g, side.low[0, n], side.low[1, n])
            for a in range(4):
                side.out[a, n] = bf16(found[a])
            side.part[0, n] = bf16(found[4])
            side.part[1, n] = bf16(found[5])

        @pl.when(jnp.logical_not(side.upper))
        def _():
            each(side, i, lower_one)
            side.send(i, 0)

        @pl.when(side.upper)
        def _():
            pair_copy(side, i, side.part).wait_recv()
            each(side, i, upper_one)
            pair_copy(side, i, side.part).start()
            side.send(i, 2)

    def finish(side, i):
        def one(n):
            for a in range(2):
                side.out[2 + a, n] = bf16(side.keep[a, n] + side.low[a, n].astype(jnp.float32))

        @pl.when(jnp.logical_not(side.upper))
        def _():
            pair_copy(side, i, side.part).wait_recv()
            each(side, i, one)
            side.send(i, 1)

    def whole(ref, semaphore):
        pltpu.make_async_copy(ref, ref, semaphore).wait()

    def arrive_row(i, pair):
        whole(row_in.at[pl.ds(2 * pair, 2), pl.ds(i * ROW_STEP, ROW_STEP)], ri_r.at[i, pair])

    def arrive_col(i, pair):
        whole(col_in.at[pl.ds(2 * pair, 2), pl.ds(i * COL_STEP, COL_STEP)], ci_r.at[i, pair])

    def arrive(i):
        arrive_row(i, 0)

        @pl.when(z_hi == 0)
        def _():
            pair_copy(row_side, i, row_in).start()

        arrive_col(i, 0)

        @pl.when(z_lo == 0)
        def _():
            pair_copy(col_side, i, col_in).start()

        arrive_row(i, 1)
        arrive_col(i, 1)

    turn_blocks(0, 0)
    pl.semaphore_wait(barrier, len(everyone))
    issue_row(0, 0)
    issue_col(0, 0)
    issue_row(0, 1)
    turn_blocks(0, 1)
    issue_col(0, 1)
    issue(1, 0)
    arrive(0)
    lax.fori_loop(2, STEPS // 2, issue, 0)
    turn_blocks(1, 0)
    turn_blocks(1, 1)
    lax.fori_loop(STEPS // 2, STEPS, issue, 0)

    def step(i, carry):
        @pl.when(i < STEPS - 1)
        def _():
            arrive(i + 1)

        @pl.when(i < STEPS)
        def _():
            for side in (row_side, col_side):
                begin(side, i)

        @pl.when(i >= LAG)
        def _():
            for side in (row_side, col_side):
                finish(side, i - LAG)

        return carry

    lax.fori_loop(0, STEPS + LAG, step, 0)

    whole(row_in.at[pl.ds(0, 3)], ri_s.at[0])
    whole(col_in.at[:, pl.ds(0, COL_BLOCK * 7 // 8)], ci_s.at[0])
    for side in (row_side, col_side):
        whole(side.low, side.f_s.at[0])

    whole(row_out.at[pl.ds(0, 3)], ro_s.at[0])
    whole(col_out.at[:, pl.ds(0, COL_BLOCK * 7 // 8)], co_s.at[0])
    whole(raw_row, ro_r.at[0])
    whole(raw_col, co_r.at[0])


def exchange(queries, keys, values, grad_output):
    bf16, f32 = jnp.bfloat16, jnp.float32
    dma = pltpu.SemaphoreType.DMA

    def side(many, length):
        return [
            pltpu.VMEM((4, many, length, LANES), bf16),
            pltpu.VMEM((2, many, length, LANES), bf16),
            pltpu.VMEM((4, many, length, LANES), bf16),
            pltpu.VMEM((2, many, length, LANES), bf16),
            pltpu.VMEM((2, many, length, LANES), f32),
        ]

    return pl.pallas_call(
        body,
        out_shape=[
            jax.ShapeDtypeStruct((4, ROWS_HERE, COLS_HERE, HALF), bf16),
            jax.ShapeDtypeStruct((4, COLS_HERE, ROWS_HERE, HALF), bf16),
        ],
        in_specs=[pl.BlockSpec(memory_space=pl.ANY)] * 4,
        out_specs=[pl.BlockSpec(memory_space=pl.ANY)] * 2,
        scratch_shapes=side(ROWS_HERE, ROW_SEQ)
        + side(COL_BLOCK, COL_SEQ)
        + [pltpu.VMEM((4, ROWS_HERE, COLS_HERE, HALF), bf16), pltpu.VMEM((4, COLS_HERE, ROWS_HERE, HALF), bf16)]
        + [dma((1,)), dma((STEPS, 2)), dma((1,)), dma((STEPS, 2))]
        + [dma((1,))] * 4
        + [dma((1,)), dma((STEPS,))] * 2
        + [dma((4, 2, 2))],
        compiler_params=pltpu.CompilerParams(
            collective_id=0, has_side_effects=True, vmem_limit_bytes=60 * 2**20
        ),
        name="exchange",
    )(queries, keys, values, grad_output)


def join_body(row_ref, col_ref, *outs):
    part = pl.program_id(1)

    @pl.when(part == 0)
    def _():
        for a in range(4):
            outs[a][...] = row_ref[a]

    @pl.when(part == 1)
    def _():
        to = lax.broadcasted_iota(jnp.int32, (256, 256), 0)
        frm = lax.broadcasted_iota(jnp.int32, (256, 256), 1)
        turn = jnp.where(frm == (to % 16) * 16 + to // 16, 1.0, 0.0).astype(jnp.bfloat16)
        for a in range(4):
            turned = dot(turn, col_ref[a].reshape(256, HALF), NN)
            outs[a][...] = turned.astype(jnp.bfloat16).reshape(16, 16, HALF)


def join(raw_row, raw_col):
    shape = jax.ShapeDtypeStruct((ROWS_HERE, COLS_HERE, 2 * HALF), jnp.bfloat16)
    return pl.pallas_call(
        join_body,
        grid=(COLS_HERE // 16, 2),
        out_shape=[shape] * 4,
        in_specs=[
            pl.BlockSpec((4, ROWS_HERE, 16, HALF), lambda i, j: (0, 0, i, 0)),
            pl.BlockSpec((4, 16, ROWS_HERE, HALF), lambda i, j: (0, i, 0, 0)),
        ],
        out_specs=[pl.BlockSpec((ROWS_HERE, 16, HALF), lambda i, j: (0, i, j))] * 4,
        compiler_params=pltpu.CompilerParams(vmem_limit_bytes=62 * 2**20),
        name="join",
    )(raw_row, raw_col)


def on_device(queries, keys, values, grad_output):
    raw_row, raw_col = exchange(queries, keys, values, grad_output)
    return tuple(join(raw_row, raw_col))


def solution(mesh):
    spec = P("row", "col", None)
    return jax.shard_map(
        on_device, mesh=mesh, in_specs=(spec,) * 4, out_specs=(spec,) * 4, check_vma=False
    )
```

```python
import functools

import jax
import jax.numpy as jnp
from jax import lax
from jax.experimental import pallas as pl
from jax.experimental.pallas import tpu as pltpu
from jax.sharding import PartitionSpec as P

MESH = pl.DeviceIdType.MESH
STEPS = 16
LAG = 1
LANES = 128
HALF = 512
ROWS_HERE = 16
COLS_HERE = 64
ROW_SEQ = 256
COL_SEQ = 128
COL_BLOCK = 32
ROW_STEP = ROWS_HERE // STEPS
COL_STEP = COL_BLOCK // STEPS
ROW_UNROLL = min(ROW_STEP, 2)
COL_UNROLL = min(COL_STEP, 4)
NT = (((1,), (1,)), ((), ()))
NN = (((1,), (0,)), ((), ()))


def dot(a, b, dims):
    return lax.dot_general(a, b, dims, preferred_element_type=jnp.float32)


def beside(first, second):
    blank = jnp.zeros_like(first)
    return jnp.concatenate(
        [jnp.concatenate([first, blank], axis=0), jnp.concatenate([blank, second], axis=0)], axis=1
    )


def per_head(lefts, rights, norms):
    length = rights[0].shape[1] // 2
    heads = (slice(0, 64), slice(64, 128))
    cols = (slice(0, length), slice(length, 2 * length))

    def with_ones(rows):
        if not norms:
            return rows
        return jnp.concatenate([rows, jnp.ones((16, rows.shape[1]), jnp.bfloat16)], axis=0)

    if length <= 128:
        both = sum(dot(with_ones(left), right, NN) for left, right in zip(lefts, rights))
        return [(both[rows, at], both[128:129, at] if norms else None) for rows, at in zip(heads, cols)]
    found = []
    for rows, at in zip(heads, cols):
        one = sum(dot(with_ones(left[rows]), right[:, at], NN) for left, right in zip(lefts, rights))
        found.append((one[:64], one[64:65] if norms else None))
    return found


def over_queries(two):
    return jnp.concatenate(two, axis=1)


def natural(two):
    return jnp.concatenate([t.astype(jnp.bfloat16) for t in two], axis=0).T


def split(pair):
    return pair[:64], pair[64:]


def attend(q, k, v, g, k_low=None, v_low=None):
    length = q.shape[0]
    keys_at = lax.broadcasted_iota(jnp.int32, (length, 2 * length), 0)
    queries_at = lax.broadcasted_iota(jnp.int32, (length, 2 * length), 1) % length
    parts = [(k, v)] if k_low is None else [(k, v), (k_low, v_low)]
    q_t = split((q * jnp.bfloat16(0.125)).T)
    g_t = split(g.T)
    flipped = [(pk.T, pv.T) for pk, pv in parts]
    q_both, g_both = beside(*q_t), beside(*g_t)
    scores = [dot(pk, q_both, NN) for pk, _ in parts]
    dprobs = [dot(pv, g_both, NN) for _, pv in parts]
    scores[0] = jnp.where(keys_at <= queries_at, scores[0], -1e30)
    top = functools.reduce(jnp.maximum, [jnp.max(s, axis=0, keepdims=True) for s in scores])
    weights = [jnp.exp(s - top) for s in scores]
    low = [w.astype(jnp.bfloat16) for w in weights]
    summed = per_head([v_t for _, v_t in flipped], low, True)
    norm = over_queries([n for _, n in summed])
    total = [t for t, _ in summed]
    scale = 1.0 / norm
    inverse = (scale[:, :length], scale[:, length:])
    attended = [t * inv for t, inv in zip(total, inverse)]
    g_here = [one.astype(jnp.float32) for one in g_t]
    delta = over_queries([jnp.sum(a * b, axis=0, keepdims=True) for a, b in zip(g_here, attended)])
    ds = [(w * (d - delta)).astype(jnp.bfloat16) for w, d in zip(weights, dprobs)]
    dq = [t * (inv * 0.125) for (t, _), inv in zip(per_head([k_t for k_t, _ in flipped], ds, False), inverse)]
    q_scaled = beside(*[(t.astype(jnp.float32) * inv).astype(jnp.bfloat16) for t, inv in zip(q_t, inverse)])
    g_scaled = beside(*[(t * inv).astype(jnp.bfloat16) for t, inv in zip(g_here, inverse)])
    found = [natural(attended), natural(dq)]
    for d, w in zip(ds, low):
        found += [dot(d, q_scaled, NT), dot(w, g_scaled, NT)]
    return found


def body(
    q_ref, k_ref, v_ref, g_ref, raw_row, raw_col,
    row_in, row_low, row_out, row_part, row_keep,
    col_in, col_low, col_out, col_part, col_keep,
    stage, send,
    ri_s, ri_r, ci_s, ci_r, ro_s, ro_r, co_s, co_r, rf_s, rf_r, cf_s, cf_r, st_l,
):
    inputs = (k_ref, v_ref, q_ref, g_ref)
    row, col = lax.axis_index("row"), lax.axis_index("col")
    z_lo, xc = row // 8, row % 8
    x, core = xc // 2, xc % 2
    z_hi, y = col // 4, col % 4

    def row_peer(d):
        other = (y + d) % 4
        return other, (row, z_hi * 4 + other)

    def col_peer(d):
        other = (xc + d) % 8
        return other, (z_lo * 8 + other, col)

    row_partner = (row, (1 - z_hi) * 4 + y)
    col_partner = ((1 - z_lo) * 8 + xc, col)

    def stage_copy(a, part, core_of):
        at = pl.ds(core_of * COL_BLOCK + part * 16, 16)
        return pltpu.make_async_copy(
            inputs[a].at[:, at, pl.ds(HALF, HALF)], stage.at[a, :, at], st_l.at[a, part, core_of]
        )

    for part in range(2):
        for a in range(4):
            for core_of in range(2):
                stage_copy(a, part, core_of).start()

    barrier = pltpu.get_barrier_semaphore()
    everyone = [row_peer(d)[1] for d in range(1, 4)] + [col_peer(d)[1] for d in range(1, 8)]
    everyone += [row_partner, col_partner]
    for device in everyone:
        pl.semaphore_signal(barrier, inc=1, device_id=device, device_id_type=MESH)

    def lanes(i):
        return pl.ds(pl.multiple_of(i * LANES, LANES), LANES)

    def row_in_copy(i, a, d):
        other, device = row_peer(d)
        return pltpu.make_async_remote_copy(
            inputs[a].at[pl.ds(i * ROW_STEP, ROW_STEP), :, lanes(other)],
            row_in.at[a, pl.ds(i * ROW_STEP, ROW_STEP), pl.ds(y * COLS_HERE, COLS_HERE)],
            ri_s.at[0], ri_r.at[i, a // 2], device_id=device, device_id_type=MESH,
        )

    def row_in_own(i, a):
        return pltpu.make_async_copy(
            inputs[a].at[pl.ds(i * ROW_STEP, ROW_STEP), :, lanes(y)],
            row_in.at[a, pl.ds(i * ROW_STEP, ROW_STEP), pl.ds(y * COLS_HERE, COLS_HERE)],
            ri_r.at[i, a // 2],
        )

    def col_in_copy(i, pair, d):
        other, device = col_peer(d)
        return pltpu.make_async_remote_copy(
            send.at[pl.ds(2 * pair, 2), pl.ds((other % 2) * COL_BLOCK + i * COL_STEP, COL_STEP), :, lanes(other // 2)],
            col_in.at[pl.ds(2 * pair, 2), pl.ds(i * COL_STEP, COL_STEP), pl.ds(xc * ROWS_HERE, ROWS_HERE)],
            ci_s.at[0], ci_r.at[i, pair], device_id=device, device_id_type=MESH,
        )

    def col_in_own(i, pair):
        return pltpu.make_async_copy(
            send.at[pl.ds(2 * pair, 2), pl.ds(core * COL_BLOCK + i * COL_STEP, COL_STEP), :, lanes(x)],
            col_in.at[pl.ds(2 * pair, 2), pl.ds(i * COL_STEP, COL_STEP), pl.ds(xc * ROWS_HERE, ROWS_HERE)],
            ci_r.at[i, pair],
        )

    def which(part):
        return pl.ds(0, 4) if part == 2 else pl.ds(2 * part, 2)

    def row_out_copy(i, part, d):
        other, device = row_peer(d)
        return pltpu.make_async_remote_copy(
            row_out.at[which(part), pl.ds(i * ROW_STEP, ROW_STEP), pl.ds(other * COLS_HERE, COLS_HERE)],
            raw_row.at[which(part), pl.ds(i * ROW_STEP, ROW_STEP), :, lanes(y)],
            ro_s.at[0], ro_r.at[0], device_id=device, device_id_type=MESH,
        )

    def row_out_own(i, part):
        return pltpu.make_async_copy(
            row_out.at[which(part), pl.ds(i * ROW_STEP, ROW_STEP), pl.ds(y * COLS_HERE, COLS_HERE)],
            raw_row.at[which(part), pl.ds(i * ROW_STEP, ROW_STEP), :, lanes(y)],
            ro_r.at[0],
        )

    def col_out_copy(i, part, d):
        other, device = col_peer(d)
        return pltpu.make_async_remote_copy(
            col_out.at[which(part), pl.ds(i * COL_STEP, COL_STEP), pl.ds(other * ROWS_HERE, ROWS_HERE)],
            raw_col.at[which(part), pl.ds(core * COL_BLOCK + i * COL_STEP, COL_STEP), :, lanes(x)],
            co_s.at[0], co_r.at[0], device_id=device, device_id_type=MESH,
        )

    def col_out_own(i, part):
        return pltpu.make_async_copy(
            col_out.at[which(part), pl.ds(i * COL_STEP, COL_STEP), pl.ds(xc * ROWS_HERE, ROWS_HERE)],
            raw_col.at[which(part), pl.ds(core * COL_BLOCK + i * COL_STEP, COL_STEP), :, lanes(x)],
            co_r.at[0],
        )

    class Side:
        pass

    def make_side(**fields):
        side = Side()
        for name, value in fields.items():
            setattr(side, name, value)
        return side

    def pair_copy(side, i, source):
        return pltpu.make_async_remote_copy(
            source.at[pl.ds(0, 2), pl.ds(i * side.step, side.step)],
            side.low.at[:, pl.ds(i * side.step, side.step)],
            side.f_s.at[0], side.f_r.at[i], device_id=side.partner, device_id_type=MESH,
        )

    def issue_row(i, pair):
        for a in (2 * pair, 2 * pair + 1):
            for d in (2, 1, 3):
                row_in_copy(i, a, d).start()
            row_in_own(i, a).start()

    def turn_blocks(part, pair):
        for a in (2 * pair, 2 * pair + 1):
            for core_of in range(2):
                stage_copy(a, part, core_of).wait()
                at = core_of * COL_BLOCK + part * 16
                send[a, pl.ds(at, 16)] = jnp.swapaxes(stage[a, :, pl.ds(at, 16), :], 0, 1)

    def issue_col(i, pair):
        for d in (4, 5, 2, 3, 6, 7, 1):
            col_in_copy(i, pair, d).start()
        col_in_own(i, pair).start()

    def issue(i, carry):
        for pair in range(2):
            issue_row(i, pair)
            issue_col(i, pair)
        return carry

    def send_row(i, part):
        for d in (2, 1, 3):
            row_out_copy(i, part, d).start()
        row_out_own(i, part).start()

    def send_col(i, part):
        for d in (4, 5, 2, 3, 6, 7, 1):
            col_out_copy(i, part, d).start()
        col_out_own(i, part).start()

    row_side = make_side(
        upper=z_hi == 1, step=ROW_STEP, unroll=ROW_UNROLL, length=ROW_SEQ, partner=row_partner,
        box=row_in, low=row_low, out=row_out, part=row_part, keep=row_keep, f_s=rf_s, f_r=rf_r,
        send=send_row,
    )
    col_side = make_side(
        upper=z_lo == 1, step=COL_STEP, unroll=COL_UNROLL, length=COL_SEQ, partner=col_partner,
        box=col_in, low=col_low, out=col_out, part=col_part, keep=col_keep, f_s=cf_s, f_r=cf_r,
        send=send_col,
    )

    def each(side, i, one):
        def some(m, carry):
            for u in range(side.unroll):
                one(i * side.step + m * side.unroll + u)
            return carry

        lax.fori_loop(0, side.step // side.unroll, some, 0)

    def bf16(value):
        return value.astype(jnp.bfloat16)

    def begin(side, i, upper):
        def lower_one(n):
            k, v, q, g = [side.box[a, n] for a in range(4)]
            found = attend(q, k, v, g)
            side.out[0, n] = found[0]
            side.out[1, n] = found[1]
            side.keep[0, n] = found[2]
            side.keep[1, n] = found[3]

        def upper_one(n):
            k, v, q, g = [side.box[a, n] for a in range(4)]
            found = attend(q, k, v, g, side.low[0, n], side.low[1, n])
            for a in range(4):
                side.out[a, n] = bf16(found[a])
            side.part[0, n] = bf16(found[4])
            side.part[1, n] = bf16(found[5])

        @pl.when(jnp.logical_not(side.upper) if not upper else side.upper)
        def _():
            if not upper:
                each(side, i, lower_one)
                side.send(i, 0)
                return
            pair_copy(side, i, side.part).wait_recv()
            each(side, i, upper_one)
            pair_copy(side, i, side.part).start()
            side.send(i, 2)

    def finish(side, i):
        def one(n):
            for a in range(2):
                side.out[2 + a, n] = bf16(side.keep[a, n] + side.low[a, n].astype(jnp.float32))

        @pl.when(jnp.logical_not(side.upper))
        def _():
            pair_copy(side, i, side.part).wait_recv()
            each(side, i, one)
            side.send(i, 1)

    def whole(ref, semaphore):
        pltpu.make_async_copy(ref, ref, semaphore).wait()

    def arrive_row(i, pair):
        whole(row_in.at[pl.ds(2 * pair, 2), pl.ds(i * ROW_STEP, ROW_STEP)], ri_r.at[i, pair])

    def arrive_col(i, pair):
        whole(col_in.at[pl.ds(2 * pair, 2), pl.ds(i * COL_STEP, COL_STEP)], ci_r.at[i, pair])

    def arrive(i, carry):
        arrive_row(i, 0)

        @pl.when(z_hi == 0)
        def _():
            pair_copy(row_side, i, row_in).start()

        arrive_col(i, 0)

        @pl.when(z_lo == 0)
        def _():
            pair_copy(col_side, i, col_in).start()

        arrive_row(i, 1)
        arrive_col(i, 1)
        return carry

    turn_blocks(0, 0)
    pl.semaphore_wait(barrier, len(everyone))
    issue_row(0, 0)
    issue_col(0, 0)
    issue_row(0, 1)
    turn_blocks(0, 1)
    issue_col(0, 1)
    issue(1, 0)
    arrive(0, 0)
    lax.fori_loop(2, STEPS // 2, issue, 0)
    turn_blocks(1, 0)
    turn_blocks(1, 1)
    lax.fori_loop(STEPS // 2, STEPS, issue, 0)

    both_upper = jnp.logical_and(z_hi == 1, z_lo == 1)

    def until(i):
        return jnp.minimum(jnp.where(both_upper, i + 2, 2 * i + 3), STEPS)

    def step(i, carry):
        lax.fori_loop(jnp.where(both_upper, i + 1, 2 * i + 1), until(i), arrive, 0)

        @pl.when(i < STEPS)
        def _():
            for upper in (False, True):
                for side in (row_side, col_side):
                    begin(side, i, upper)

        @pl.when(i >= LAG)
        def _():
            for side in (row_side, col_side):
                finish(side, i - LAG)

        return carry

    lax.fori_loop(0, STEPS + LAG, step, 0)

    whole(row_in.at[pl.ds(0, 3)], ri_s.at[0])
    whole(col_in.at[:, pl.ds(0, COL_BLOCK * 7 // 8)], ci_s.at[0])
    for side in (row_side, col_side):
        whole(side.low, side.f_s.at[0])

    whole(row_out.at[pl.ds(0, 3)], ro_s.at[0])
    whole(col_out.at[:, pl.ds(0, COL_BLOCK * 7 // 8)], co_s.at[0])
    whole(raw_row, ro_r.at[0])
    whole(raw_col, co_r.at[0])


def exchange(queries, keys, values, grad_output):
    bf16, f32 = jnp.bfloat16, jnp.float32
    dma = pltpu.SemaphoreType.DMA

    def side(many, length):
        return [
            pltpu.VMEM((4, many, length, LANES), bf16),
            pltpu.VMEM((2, many, length, LANES), bf16),
            pltpu.VMEM((4, many, length, LANES), bf16),
            pltpu.VMEM((2, many, length, LANES), bf16),
            pltpu.VMEM((2, many, length, LANES), f32),
        ]

    return pl.pallas_call(
        body,
        out_shape=[
            jax.ShapeDtypeStruct((4, ROWS_HERE, COLS_HERE, HALF), bf16),
            jax.ShapeDtypeStruct((4, COLS_HERE, ROWS_HERE, HALF), bf16),
        ],
        in_specs=[pl.BlockSpec(memory_space=pl.ANY)] * 4,
        out_specs=[pl.BlockSpec(memory_space=pl.ANY)] * 2,
        scratch_shapes=side(ROWS_HERE, ROW_SEQ)
        + side(COL_BLOCK, COL_SEQ)
        + [pltpu.VMEM((4, ROWS_HERE, COLS_HERE, HALF), bf16), pltpu.VMEM((4, COLS_HERE, ROWS_HERE, HALF), bf16)]
        + [dma((1,)), dma((STEPS, 2)), dma((1,)), dma((STEPS, 2))]
        + [dma((1,))] * 4
        + [dma((1,)), dma((STEPS,))] * 2
        + [dma((4, 2, 2))],
        compiler_params=pltpu.CompilerParams(
            collective_id=0, has_side_effects=True, vmem_limit_bytes=60 * 2**20
        ),
        name="exchange",
    )(queries, keys, values, grad_output)


def join_body(row_ref, col_ref, out_0, out_1, out_2, out_3, rows, cols, turned, row_in, row_out, col_in, col_out):
    outs = (out_0, out_1, out_2, out_3)
    blocks = COLS_HERE // 16

    def load_row(a):
        return pltpu.make_async_copy(row_ref.at[a], rows.at[a], row_in.at[a])

    def store_row(a):
        return pltpu.make_async_copy(rows.at[a], outs[a].at[:, :, pl.ds(0, HALF)], row_out.at[a])

    def load_col(a, b):
        at = pl.ds(b * 16, 16)
        return pltpu.make_async_copy(col_ref.at[a, at], cols.at[a, at], col_in.at[a, b])

    def store_col(a, b):
        at = pl.ds(b * 16, 16)
        return pltpu.make_async_copy(turned.at[a, :, at], outs[a].at[:, at, pl.ds(HALF, HALF)], col_out.at[a, b])

    for a in range(4):
        for b in range(blocks):
            load_col(a, b).start()
        load_row(a).start()
    for a in range(4):
        for b in range(blocks):
            load_col(a, b).wait()
            at = pl.ds(b * 16, 16)
            turned[a, :, at] = jnp.swapaxes(cols[a, at], 0, 1)
            store_col(a, b).start()
        load_row(a).wait()
        store_row(a).start()
    for a in range(4):
        for b in range(blocks):
            store_col(a, b).wait()
        store_row(a).wait()


def join(raw_row, raw_col):
    shape = jax.ShapeDtypeStruct((ROWS_HERE, COLS_HERE, 2 * HALF), jnp.bfloat16)
    dma = pltpu.SemaphoreType.DMA
    return pl.pallas_call(
        join_body,
        out_shape=[shape] * 4,
        in_specs=[pl.BlockSpec(memory_space=pl.ANY)] * 2,
        out_specs=[pl.BlockSpec(memory_space=pl.ANY)] * 4,
        scratch_shapes=[
            pltpu.VMEM((4, ROWS_HERE, COLS_HERE, HALF), jnp.bfloat16),
            pltpu.VMEM((4, COLS_HERE, ROWS_HERE, HALF), jnp.bfloat16),
            pltpu.VMEM((4, ROWS_HERE, COLS_HERE, HALF), jnp.bfloat16),
            dma((4,)), dma((4,)), dma((4, COLS_HERE // 16)), dma((4, COLS_HERE // 16)),
        ],
        compiler_params=pltpu.CompilerParams(vmem_limit_bytes=62 * 2**20),
        name="join",
    )(raw_row, raw_col)


def on_device(queries, keys, values, grad_output):
    raw_row, raw_col = exchange(queries, keys, values, grad_output)
    return tuple(join(raw_row, raw_col))


def solution(mesh):
    spec = P("row", "col", None)
    return jax.shard_map(
        on_device, mesh=mesh, in_specs=(spec,) * 4, out_specs=(spec,) * 4, check_vma=False
    )
```

```python
import functools

import jax
import jax.numpy as jnp
from jax import lax
from jax.experimental import pallas as pl
from jax.experimental.pallas import tpu as pltpu
from jax.sharding import PartitionSpec as P

MESH = pl.DeviceIdType.MESH
STEPS = 16
AHEAD = 4
LAG, LONG_LAG = 1, 5
LANES = 128
HALF = 512
ROWS_HERE = 16
COLS_HERE = 64
ROW_SEQ = 256
COL_SEQ = 128
COL_BLOCK = 32
ROW_STEP = ROWS_HERE // STEPS
COL_STEP = COL_BLOCK // STEPS
ROW_UNROLL = min(ROW_STEP, 2)
COL_UNROLL = min(COL_STEP, 4)
NT = (((1,), (1,)), ((), ()))
NN = (((1,), (0,)), ((), ()))


def dot(a, b, dims):
    return lax.dot_general(a, b, dims, preferred_element_type=jnp.float32)


def beside(first, second):
    blank = jnp.zeros_like(first)
    return jnp.concatenate(
        [jnp.concatenate([first, blank], axis=0), jnp.concatenate([blank, second], axis=0)], axis=1
    )


def per_head(lefts, rights, norms):
    length = rights[0].shape[1] // 2
    heads = (slice(0, 64), slice(64, 128))
    cols = (slice(0, length), slice(length, 2 * length))

    def with_ones(rows):
        if not norms:
            return rows
        return jnp.concatenate([rows, jnp.ones((16, rows.shape[1]), jnp.bfloat16)], axis=0)

    if length <= 128:
        both = sum(dot(with_ones(left), right, NN) for left, right in zip(lefts, rights))
        return [(both[rows, at], both[128:129, at] if norms else None) for rows, at in zip(heads, cols)]
    found = []
    for rows, at in zip(heads, cols):
        one = sum(dot(with_ones(left[rows]), right[:, at], NN) for left, right in zip(lefts, rights))
        found.append((one[:64], one[64:65] if norms else None))
    return found


def over_queries(two):
    return jnp.concatenate(two, axis=1)


def natural(two):
    return jnp.concatenate([t.astype(jnp.bfloat16) for t in two], axis=0).T


def split(pair):
    return pair[:64], pair[64:]


def attend(q, k, v, g, k_low=None, v_low=None):
    length = q.shape[0]
    keys_at = lax.broadcasted_iota(jnp.int32, (length, 2 * length), 0)
    queries_at = lax.broadcasted_iota(jnp.int32, (length, 2 * length), 1) % length
    parts = [(k, v)] if k_low is None else [(k, v), (k_low, v_low)]
    q_t = split((q * jnp.bfloat16(0.125)).T)
    g_t = split(g.T)
    flipped = [(pk.T, pv.T) for pk, pv in parts]
    q_both, g_both = beside(*q_t), beside(*g_t)
    scores = [dot(pk, q_both, NN) for pk, _ in parts]
    dprobs = [dot(pv, g_both, NN) for _, pv in parts]
    scores[0] = jnp.where(keys_at <= queries_at, scores[0], -1e30)
    top = functools.reduce(jnp.maximum, [jnp.max(s, axis=0, keepdims=True) for s in scores])
    weights = [jnp.exp(s - top) for s in scores]
    low = [w.astype(jnp.bfloat16) for w in weights]
    summed = per_head([v_t for _, v_t in flipped], low, True)
    norm = over_queries([n for _, n in summed])
    total = [t for t, _ in summed]
    scale = 1.0 / norm
    inverse = (scale[:, :length], scale[:, length:])
    attended = [t * inv for t, inv in zip(total, inverse)]
    g_here = [one.astype(jnp.float32) for one in g_t]
    delta = over_queries([jnp.sum(a * b, axis=0, keepdims=True) for a, b in zip(g_here, attended)])
    ds = [(w * (d - delta)).astype(jnp.bfloat16) for w, d in zip(weights, dprobs)]
    dq = [t * (inv * 0.125) for (t, _), inv in zip(per_head([k_t for k_t, _ in flipped], ds, False), inverse)]
    q_scaled = beside(*[(t.astype(jnp.float32) * inv).astype(jnp.bfloat16) for t, inv in zip(q_t, inverse)])
    g_scaled = beside(*[(t * inv).astype(jnp.bfloat16) for t, inv in zip(g_here, inverse)])
    found = [natural(attended), natural(dq)]
    for d, w in zip(ds, low):
        found += [dot(d, q_scaled, NT), dot(w, g_scaled, NT)]
    return found


def body(
    q_ref, k_ref, v_ref, g_ref, raw_row, raw_col,
    row_in, row_low, row_out, row_part, row_keep,
    col_in, col_low, col_out, col_part, col_keep,
    stage, send,
    ri_s, ri_r, ci_s, ci_r, ro_s, ro_r, co_s, co_r, rf_s, rf_r, cf_s, cf_r, st_l,
):
    inputs = (k_ref, v_ref, q_ref, g_ref)
    row, col = lax.axis_index("row"), lax.axis_index("col")
    z_lo, xc = row // 8, row % 8
    x, core = xc // 2, xc % 2
    z_hi, y = col // 4, col % 4

    def row_peer(d):
        other = (y + d) % 4
        return other, (row, z_hi * 4 + other)

    def col_peer(d):
        other = (xc + d) % 8
        return other, (z_lo * 8 + other, col)

    row_partner = (row, (1 - z_hi) * 4 + y)
    col_partner = ((1 - z_lo) * 8 + xc, col)

    def stage_copy(a, part, core_of):
        at = pl.ds(core_of * COL_BLOCK + part * 16, 16)
        return pltpu.make_async_copy(
            inputs[a].at[:, at, pl.ds(HALF, HALF)], stage.at[a, :, at], st_l.at[a, part, core_of]
        )


    barrier = pltpu.get_barrier_semaphore()
    everyone = [row_peer(d)[1] for d in range(1, 4)] + [col_peer(d)[1] for d in range(1, 8)]
    everyone += [row_partner, col_partner]
    for device in everyone:
        pl.semaphore_signal(barrier, inc=1, device_id=device, device_id_type=MESH)

    def lanes(i):
        return pl.ds(pl.multiple_of(i * LANES, LANES), LANES)

    def row_in_copy(i, a, d):
        other, device = row_peer(d)
        return pltpu.make_async_remote_copy(
            inputs[a].at[pl.ds(i * ROW_STEP, ROW_STEP), :, lanes(other)],
            row_in.at[a, pl.ds(i * ROW_STEP, ROW_STEP), pl.ds(y * COLS_HERE, COLS_HERE)],
            ri_s.at[0], ri_r.at[i, a // 2], device_id=device, device_id_type=MESH,
        )

    def row_in_own(i, a):
        return pltpu.make_async_copy(
            inputs[a].at[pl.ds(i * ROW_STEP, ROW_STEP), :, lanes(y)],
            row_in.at[a, pl.ds(i * ROW_STEP, ROW_STEP), pl.ds(y * COLS_HERE, COLS_HERE)],
            ri_r.at[i, a // 2],
        )

    def col_in_copy(i, pair, d):
        other, device = col_peer(d)
        return pltpu.make_async_remote_copy(
            send.at[pl.ds(2 * pair, 2), pl.ds((other % 2) * COL_BLOCK + i * COL_STEP, COL_STEP), :, lanes(other // 2)],
            col_in.at[pl.ds(2 * pair, 2), pl.ds(i * COL_STEP, COL_STEP), pl.ds(xc * ROWS_HERE, ROWS_HERE)],
            ci_s.at[0], ci_r.at[i, pair], device_id=device, device_id_type=MESH,
        )

    def col_in_own(i, pair):
        return pltpu.make_async_copy(
            send.at[pl.ds(2 * pair, 2), pl.ds(core * COL_BLOCK + i * COL_STEP, COL_STEP), :, lanes(x)],
            col_in.at[pl.ds(2 * pair, 2), pl.ds(i * COL_STEP, COL_STEP), pl.ds(xc * ROWS_HERE, ROWS_HERE)],
            ci_r.at[i, pair],
        )

    def which(part):
        return pl.ds(0, 4) if part == 2 else pl.ds(2 * part, 2)

    def row_out_copy(i, part, d):
        other, device = row_peer(d)
        return pltpu.make_async_remote_copy(
            row_out.at[which(part), pl.ds(i * ROW_STEP, ROW_STEP), pl.ds(other * COLS_HERE, COLS_HERE)],
            raw_row.at[which(part), pl.ds(i * ROW_STEP, ROW_STEP), :, lanes(y)],
            ro_s.at[0], ro_r.at[0], device_id=device, device_id_type=MESH,
        )

    def row_out_own(i, part):
        return pltpu.make_async_copy(
            row_out.at[which(part), pl.ds(i * ROW_STEP, ROW_STEP), pl.ds(y * COLS_HERE, COLS_HERE)],
            raw_row.at[which(part), pl.ds(i * ROW_STEP, ROW_STEP), :, lanes(y)],
            ro_r.at[0],
        )

    def col_out_copy(i, part, d):
        other, device = col_peer(d)
        return pltpu.make_async_remote_copy(
            col_out.at[which(part), pl.ds(i * COL_STEP, COL_STEP), pl.ds(other * ROWS_HERE, ROWS_HERE)],
            raw_col.at[which(part), pl.ds(core * COL_BLOCK + i * COL_STEP, COL_STEP), :, lanes(x)],
            co_s.at[0], co_r.at[0], device_id=device, device_id_type=MESH,
        )

    def col_out_own(i, part):
        return pltpu.make_async_copy(
            col_out.at[which(part), pl.ds(i * COL_STEP, COL_STEP), pl.ds(xc * ROWS_HERE, ROWS_HERE)],
            raw_col.at[which(part), pl.ds(core * COL_BLOCK + i * COL_STEP, COL_STEP), :, lanes(x)],
            co_r.at[0],
        )

    class Side:
        pass

    def make_side(**fields):
        side = Side()
        for name, value in fields.items():
            setattr(side, name, value)
        return side

    def pair_copy(side, i, source):
        return pltpu.make_async_remote_copy(
            source.at[pl.ds(0, 2), pl.ds(i * side.step, side.step)],
            side.low.at[:, pl.ds(i * side.step, side.step)],
            side.f_s.at[0], side.f_r.at[i], device_id=side.partner, device_id_type=MESH,
        )

    def ahead_copy(i, a):
        return pltpu.make_async_remote_copy(
            inputs[a].at[pl.ds(i * ROW_STEP, ROW_STEP), :, lanes(y)],
            row_low.at[a, pl.ds(i * ROW_STEP, ROW_STEP), pl.ds(y * COLS_HERE, COLS_HERE)],
            rf_s.at[0], rf_r.at[i], device_id=row_partner, device_id_type=MESH,
        )

    def rest_copy(i, d):
        columns = pl.ds((y + d) % 4 * COLS_HERE, COLS_HERE)
        return pltpu.make_async_remote_copy(
            row_in.at[pl.ds(0, 2), pl.ds(i * ROW_STEP, ROW_STEP), columns],
            row_low.at[:, pl.ds(i * ROW_STEP, ROW_STEP), columns],
            rf_s.at[0], rf_r.at[i], device_id=row_partner, device_id_type=MESH,
        )

    def issue_row(i, pair):
        for a in (2 * pair, 2 * pair + 1):
            for d in (2, 1, 3):
                row_in_copy(i, a, d).start()
            row_in_own(i, a).start()

    def turn_blocks(part, pair):
        for a in (2 * pair, 2 * pair + 1):
            for core_of in range(2):
                stage_copy(a, part, core_of).wait()
                at = core_of * COL_BLOCK + part * 16
                send[a, pl.ds(at, 16)] = jnp.swapaxes(stage[a, :, pl.ds(at, 16), :], 0, 1)

    def issue_col(i, pair):
        for d in (4, 5, 2, 3, 6, 7, 1):
            col_in_copy(i, pair, d).start()
        col_in_own(i, pair).start()

    def issue(i, carry):
        for pair in range(2):
            issue_row(i, pair)
            issue_col(i, pair)
        return carry

    def send_row(i, part):
        for d in (2, 1, 3):
            row_out_copy(i, part, d).start()
        row_out_own(i, part).start()

    def send_col(i, part):
        for d in (4, 5, 2, 3, 6, 7, 1):
            col_out_copy(i, part, d).start()
        col_out_own(i, part).start()

    row_side = make_side(
        upper=z_hi == 1, step=ROW_STEP, unroll=ROW_UNROLL, length=ROW_SEQ, partner=row_partner,
        box=row_in, low=row_low, out=row_out, part=row_part, keep=row_keep, f_s=rf_s, f_r=rf_r,
        send=send_row,
    )
    col_side = make_side(
        upper=z_lo == 1, step=COL_STEP, unroll=COL_UNROLL, length=COL_SEQ, partner=col_partner,
        box=col_in, low=col_low, out=col_out, part=col_part, keep=col_keep, f_s=cf_s, f_r=cf_r,
        send=send_col,
    )

    def each(side, i, one):
        def some(m, carry):
            for u in range(side.unroll):
                one(i * side.step + m * side.unroll + u)
            return carry

        lax.fori_loop(0, side.step // side.unroll, some, 0)

    def bf16(value):
        return value.astype(jnp.bfloat16)

    def begin(side, i, upper):
        def lower_one(n):
            k, v, q, g = [side.box[a, n] for a in range(4)]
            found = attend(q, k, v, g)
            side.out[0, n] = found[0]
            side.out[1, n] = found[1]
            side.keep[0, n] = found[2]
            side.keep[1, n] = found[3]

        def upper_one(n):
            k, v, q, g = [side.box[a, n] for a in range(4)]
            found = attend(q, k, v, g, side.low[0, n], side.low[1, n])
            for a in range(4):
                side.out[a, n] = bf16(found[a])
            side.part[0, n] = bf16(found[4])
            side.part[1, n] = bf16(found[5])

        @pl.when(jnp.logical_not(side.upper) if not upper else side.upper)
        def _():
            if not upper:
                each(side, i, lower_one)
                side.send(i, 0)
                return
            pair_copy(side, i, side.part).wait_recv()
            each(side, i, upper_one)
            pair_copy(side, i, side.part).start()
            side.send(i, 2)

    def finish(side, i):
        def one(n):
            for a in range(2):
                side.out[2 + a, n] = bf16(side.keep[a, n] + side.low[a, n].astype(jnp.float32))

        @pl.when(jnp.logical_not(side.upper))
        def _():
            pair_copy(side, i, side.part).wait_recv()
            each(side, i, one)
            side.send(i, 1)

    def whole(ref, semaphore):
        pltpu.make_async_copy(ref, ref, semaphore).wait()

    def arrive_row(i, pair):
        whole(row_in.at[pl.ds(2 * pair, 2), pl.ds(i * ROW_STEP, ROW_STEP)], ri_r.at[i, pair])

    def arrive_col(i, pair):
        whole(col_in.at[pl.ds(2 * pair, 2), pl.ds(i * COL_STEP, COL_STEP)], ci_r.at[i, pair])

    def arrive(i, carry):
        arrive_row(i, 0)

        @pl.when(z_hi == 0)
        def _():
            @pl.when(i < AHEAD)
            def _():
                for d in range(1, 4):
                    rest_copy(i, d).start()

            @pl.when(i >= AHEAD)
            def _():
                pair_copy(row_side, i, row_in).start()

        arrive_col(i, 0)

        @pl.when(z_lo == 0)
        def _():
            pair_copy(col_side, i, col_in).start()

        arrive_row(i, 1)
        arrive_col(i, 1)
        return carry

    def stage_part(part):
        for a in range(4):
            for core_of in range(2):
                stage_copy(a, part, core_of).start()

    stage_part(0)
    turn_blocks(0, 0)
    pl.semaphore_wait(barrier, len(everyone))
    issue_row(0, 0)

    @pl.when(z_hi == 0)
    def _():
        for i in range(AHEAD):
            for a in range(2):
                ahead_copy(i, a).start()

    issue_col(0, 0)
    issue_row(0, 1)
    turn_blocks(0, 1)
    issue_col(0, 1)
    issue(1, 0)
    stage_part(1)
    arrive(0, 0)
    lax.fori_loop(2, 4, issue, 0)

    both_upper = jnp.logical_and(z_hi == 1, z_lo == 1)
    lag = jnp.where(z_hi + z_lo == 0, LONG_LAG, LAG)

    def until(i):
        return jnp.minimum(jnp.where(both_upper, i + 1, 2 * i + 3), STEPS)

    def step(i, carry):
        @pl.when(i == STEPS // 4 - 2)
        def _():
            turn_blocks(1, 0)
            turn_blocks(1, 1)

        lax.fori_loop(2 * i + 4, jnp.minimum(2 * i + 6, STEPS), issue, 0)
        lax.fori_loop(jnp.where(both_upper, jnp.maximum(i, 1), 2 * i + 1), until(i), arrive, 0)

        @pl.when(i < STEPS)
        def _():
            for upper in (False, True):
                for side in (row_side, col_side):
                    begin(side, i, upper)

        @pl.when(jnp.logical_and(i >= lag, i < STEPS + lag))
        def _():
            for side in (row_side, col_side):
                finish(side, i - lag)

        return carry

    lax.fori_loop(0, STEPS + LONG_LAG, step, 0)

    whole(row_in.at[pl.ds(0, 3)], ri_s.at[0])
    whole(col_in.at[:, pl.ds(0, COL_BLOCK * 7 // 8)], ci_s.at[0])
    for side in (row_side, col_side):
        whole(side.low, side.f_s.at[0])

    whole(row_out.at[pl.ds(0, 3)], ro_s.at[0])
    whole(col_out.at[:, pl.ds(0, COL_BLOCK * 7 // 8)], co_s.at[0])
    whole(raw_row, ro_r.at[0])
    whole(raw_col, co_r.at[0])


def exchange(queries, keys, values, grad_output):
    bf16, f32 = jnp.bfloat16, jnp.float32
    dma = pltpu.SemaphoreType.DMA

    def side(many, length):
        return [
            pltpu.VMEM((4, many, length, LANES), bf16),
            pltpu.VMEM((2, many, length, LANES), bf16),
            pltpu.VMEM((4, many, length, LANES), bf16),
            pltpu.VMEM((2, many, length, LANES), bf16),
            pltpu.VMEM((2, many, length, LANES), f32),
        ]

    return pl.pallas_call(
        body,
        out_shape=[
            jax.ShapeDtypeStruct((4, ROWS_HERE, COLS_HERE, HALF), bf16),
            jax.ShapeDtypeStruct((4, COLS_HERE, ROWS_HERE, HALF), bf16),
        ],
        in_specs=[pl.BlockSpec(memory_space=pl.ANY)] * 4,
        out_specs=[pl.BlockSpec(memory_space=pl.ANY)] * 2,
        scratch_shapes=side(ROWS_HERE, ROW_SEQ)
        + side(COL_BLOCK, COL_SEQ)
        + [pltpu.VMEM((4, ROWS_HERE, COLS_HERE, HALF), bf16), pltpu.VMEM((4, COLS_HERE, ROWS_HERE, HALF), bf16)]
        + [dma((1,)), dma((STEPS, 2)), dma((1,)), dma((STEPS, 2))]
        + [dma((1,))] * 4
        + [dma((1,)), dma((STEPS,))] * 2
        + [dma((4, 2, 2))],
        compiler_params=pltpu.CompilerParams(
            collective_id=0, has_side_effects=True, vmem_limit_bytes=60 * 2**20
        ),
        name="exchange",
    )(queries, keys, values, grad_output)


def join_body(row_ref, col_ref, out_0, out_1, out_2, out_3, rows, cols, turned, row_in, row_out, col_in, col_out):
    outs = (out_0, out_1, out_2, out_3)
    blocks = COLS_HERE // 16

    def load_row(a):
        return pltpu.make_async_copy(row_ref.at[a], rows.at[a], row_in.at[a])

    def store_row(a):
        return pltpu.make_async_copy(rows.at[a], outs[a].at[:, :, pl.ds(0, HALF)], row_out.at[a])

    def load_col(a, b):
        at = pl.ds(b * 16, 16)
        return pltpu.make_async_copy(col_ref.at[a, at], cols.at[a, at], col_in.at[a, b])

    def store_col(a, b):
        at = pl.ds(b * 16, 16)
        return pltpu.make_async_copy(turned.at[a, :, at], outs[a].at[:, at, pl.ds(HALF, HALF)], col_out.at[a, b])

    for a in range(4):
        for b in range(blocks):
            load_col(a, b).start()
        load_row(a).start()
    for a in range(4):
        for b in range(blocks):
            load_col(a, b).wait()
            at = pl.ds(b * 16, 16)
            turned[a, :, at] = jnp.swapaxes(cols[a, at], 0, 1)
            store_col(a, b).start()
        load_row(a).wait()
        store_row(a).start()
    for a in range(4):
        for b in range(blocks):
            store_col(a, b).wait()
        store_row(a).wait()


def join(raw_row, raw_col):
    shape = jax.ShapeDtypeStruct((ROWS_HERE, COLS_HERE, 2 * HALF), jnp.bfloat16)
    dma = pltpu.SemaphoreType.DMA
    return pl.pallas_call(
        join_body,
        out_shape=[shape] * 4,
        in_specs=[pl.BlockSpec(memory_space=pl.ANY)] * 2,
        out_specs=[pl.BlockSpec(memory_space=pl.ANY)] * 4,
        scratch_shapes=[
            pltpu.VMEM((4, ROWS_HERE, COLS_HERE, HALF), jnp.bfloat16),
            pltpu.VMEM((4, COLS_HERE, ROWS_HERE, HALF), jnp.bfloat16),
            pltpu.VMEM((4, ROWS_HERE, COLS_HERE, HALF), jnp.bfloat16),
            dma((4,)), dma((4,)), dma((4, COLS_HERE // 16)), dma((4, COLS_HERE // 16)),
        ],
        compiler_params=pltpu.CompilerParams(vmem_limit_bytes=62 * 2**20),
        name="join",
    )(raw_row, raw_col)


def on_device(queries, keys, values, grad_output):
    raw_row, raw_col = exchange(queries, keys, values, grad_output)
    return tuple(join(raw_row, raw_col))


def solution(mesh):
    spec = P("row", "col", None)
    return jax.shard_map(
        on_device, mesh=mesh, in_specs=(spec,) * 4, out_specs=(spec,) * 4, check_vma=False
    )
```

```python
import functools

import jax
import jax.numpy as jnp
from jax import lax
from jax.experimental import pallas as pl
from jax.experimental.pallas import tpu as pltpu
from jax.sharding import PartitionSpec as P

MESH = pl.DeviceIdType.MESH
STEPS = 16
AHEAD, FAR_AHEAD = 4, 8
LAG, LONG_LAG = 1, 5
LANES = 128
HALF = 512
ROWS_HERE = 16
COLS_HERE = 64
ROW_SEQ = 256
COL_SEQ = 128
COL_BLOCK = 32
ROW_STEP = ROWS_HERE // STEPS
COL_STEP = COL_BLOCK // STEPS
ROW_UNROLL = min(ROW_STEP, 2)
COL_UNROLL = min(COL_STEP, 4)
NT = (((1,), (1,)), ((), ()))
NN = (((1,), (0,)), ((), ()))


def dot(a, b, dims):
    return lax.dot_general(a, b, dims, preferred_element_type=jnp.float32)


def beside(first, second):
    blank = jnp.zeros_like(first)
    return jnp.concatenate(
        [jnp.concatenate([first, blank], axis=0), jnp.concatenate([blank, second], axis=0)], axis=1
    )


def per_head(lefts, rights, norms):
    length = rights[0].shape[1] // 2
    heads = (slice(0, 64), slice(64, 128))
    cols = (slice(0, length), slice(length, 2 * length))

    def with_ones(rows):
        if not norms:
            return rows
        return jnp.concatenate([rows, jnp.ones((16, rows.shape[1]), jnp.bfloat16)], axis=0)

    if length <= 128:
        both = sum(dot(with_ones(left), right, NN) for left, right in zip(lefts, rights))
        return [(both[rows, at], both[128:129, at] if norms else None) for rows, at in zip(heads, cols)]
    found = []
    for rows, at in zip(heads, cols):
        one = sum(dot(with_ones(left[rows]), right[:, at], NN) for left, right in zip(lefts, rights))
        found.append((one[:64], one[64:65] if norms else None))
    return found


def over_queries(two):
    return jnp.concatenate(two, axis=1)


def natural(two):
    return jnp.concatenate([t.astype(jnp.bfloat16) for t in two], axis=0).T


def split(pair):
    return pair[:64], pair[64:]


def attend(q, k, v, g, k_low=None, v_low=None):
    length = q.shape[0]
    keys_at = lax.broadcasted_iota(jnp.int32, (length, 2 * length), 0)
    queries_at = lax.broadcasted_iota(jnp.int32, (length, 2 * length), 1) % length
    parts = [(k, v)] if k_low is None else [(k, v), (k_low, v_low)]
    q_t = split((q * jnp.bfloat16(0.125)).T)
    g_t = split(g.T)
    flipped = [(pk.T, pv.T) for pk, pv in parts]
    q_both, g_both = beside(*q_t), beside(*g_t)
    scores = [dot(pk, q_both, NN) for pk, _ in parts]
    dprobs = [dot(pv, g_both, NN) for _, pv in parts]
    scores[0] = jnp.where(keys_at <= queries_at, scores[0], -1e30)
    top = functools.reduce(jnp.maximum, [jnp.max(s, axis=0, keepdims=True) for s in scores])
    weights = [jnp.exp(s - top) for s in scores]
    low = [w.astype(jnp.bfloat16) for w in weights]
    summed = per_head([v_t for _, v_t in flipped], low, True)
    norm = over_queries([n for _, n in summed])
    total = [t for t, _ in summed]
    scale = 1.0 / norm
    inverse = (scale[:, :length], scale[:, length:])
    attended = [t * inv for t, inv in zip(total, inverse)]
    g_here = [one.astype(jnp.float32) for one in g_t]
    delta = over_queries([jnp.sum(a * b, axis=0, keepdims=True) for a, b in zip(g_here, attended)])
    ds = [(w * (d - delta)).astype(jnp.bfloat16) for w, d in zip(weights, dprobs)]
    dq = [t * (inv * 0.125) for (t, _), inv in zip(per_head([k_t for k_t, _ in flipped], ds, False), inverse)]
    q_scaled = beside(*[(t.astype(jnp.float32) * inv).astype(jnp.bfloat16) for t, inv in zip(q_t, inverse)])
    g_scaled = beside(*[(t * inv).astype(jnp.bfloat16) for t, inv in zip(g_here, inverse)])
    found = [natural(attended), natural(dq)]
    for d, w in zip(ds, low):
        found += [dot(d, q_scaled, NT), dot(w, g_scaled, NT)]
    return found


def body(
    q_ref, k_ref, v_ref, g_ref, raw_row, raw_col,
    row_in, row_low, row_out, row_part, row_keep,
    col_in, col_low, col_out, col_part, col_keep,
    stage, send,
    ri_s, ri_r, ci_s, ci_r, ro_s, ro_r, co_s, co_r, rf_s, rf_r, cf_s, cf_r, st_l,
):
    inputs = (k_ref, v_ref, q_ref, g_ref)
    row, col = lax.axis_index("row"), lax.axis_index("col")
    z_lo, xc = row // 8, row % 8
    x, core = xc // 2, xc % 2
    z_hi, y = col // 4, col % 4

    def row_peer(d):
        other = (y + d) % 4
        return other, (row, z_hi * 4 + other)

    def col_peer(d):
        other = (xc + d) % 8
        return other, (z_lo * 8 + other, col)

    row_partner = (row, (1 - z_hi) * 4 + y)
    col_partner = ((1 - z_lo) * 8 + xc, col)

    def stage_copy(a, part, core_of):
        at = pl.ds(core_of * COL_BLOCK + part * 16, 16)
        return pltpu.make_async_copy(
            inputs[a].at[:, at, pl.ds(HALF, HALF)], stage.at[a, :, at], st_l.at[a, part, core_of]
        )


    barrier = pltpu.get_barrier_semaphore()
    everyone = [row_peer(d)[1] for d in range(1, 4)] + [col_peer(d)[1] for d in range(1, 8)]
    everyone += [row_partner, col_partner]
    for device in everyone:
        pl.semaphore_signal(barrier, inc=1, device_id=device, device_id_type=MESH)

    def lanes(i):
        return pl.ds(pl.multiple_of(i * LANES, LANES), LANES)

    def row_in_copy(i, a, d):
        other, device = row_peer(d)
        return pltpu.make_async_remote_copy(
            inputs[a].at[pl.ds(i * ROW_STEP, ROW_STEP), :, lanes(other)],
            row_in.at[a, pl.ds(i * ROW_STEP, ROW_STEP), pl.ds(y * COLS_HERE, COLS_HERE)],
            ri_s.at[0], ri_r.at[i, a // 2], device_id=device, device_id_type=MESH,
        )

    def row_in_own(i, a):
        return pltpu.make_async_copy(
            inputs[a].at[pl.ds(i * ROW_STEP, ROW_STEP), :, lanes(y)],
            row_in.at[a, pl.ds(i * ROW_STEP, ROW_STEP), pl.ds(y * COLS_HERE, COLS_HERE)],
            ri_r.at[i, a // 2],
        )

    def col_in_copy(i, pair, d):
        other, device = col_peer(d)
        return pltpu.make_async_remote_copy(
            send.at[pl.ds(2 * pair, 2), pl.ds((other % 2) * COL_BLOCK + i * COL_STEP, COL_STEP), :, lanes(other // 2)],
            col_in.at[pl.ds(2 * pair, 2), pl.ds(i * COL_STEP, COL_STEP), pl.ds(xc * ROWS_HERE, ROWS_HERE)],
            ci_s.at[0], ci_r.at[i, pair], device_id=device, device_id_type=MESH,
        )

    def col_in_own(i, pair):
        return pltpu.make_async_copy(
            send.at[pl.ds(2 * pair, 2), pl.ds(core * COL_BLOCK + i * COL_STEP, COL_STEP), :, lanes(x)],
            col_in.at[pl.ds(2 * pair, 2), pl.ds(i * COL_STEP, COL_STEP), pl.ds(xc * ROWS_HERE, ROWS_HERE)],
            ci_r.at[i, pair],
        )

    def which(part):
        return pl.ds(0, 4) if part == 2 else pl.ds(2 * part, 2)

    def row_out_copy(i, part, d):
        other, device = row_peer(d)
        return pltpu.make_async_remote_copy(
            row_out.at[which(part), pl.ds(i * ROW_STEP, ROW_STEP), pl.ds(other * COLS_HERE, COLS_HERE)],
            raw_row.at[which(part), pl.ds(i * ROW_STEP, ROW_STEP), :, lanes(y)],
            ro_s.at[0], ro_r.at[0], device_id=device, device_id_type=MESH,
        )

    def row_out_own(i, part):
        return pltpu.make_async_copy(
            row_out.at[which(part), pl.ds(i * ROW_STEP, ROW_STEP), pl.ds(y * COLS_HERE, COLS_HERE)],
            raw_row.at[which(part), pl.ds(i * ROW_STEP, ROW_STEP), :, lanes(y)],
            ro_r.at[0],
        )

    def col_out_copy(i, part, d):
        other, device = col_peer(d)
        return pltpu.make_async_remote_copy(
            col_out.at[which(part), pl.ds(i * COL_STEP, COL_STEP), pl.ds(other * ROWS_HERE, ROWS_HERE)],
            raw_col.at[which(part), pl.ds(core * COL_BLOCK + i * COL_STEP, COL_STEP), :, lanes(x)],
            co_s.at[0], co_r.at[0], device_id=device, device_id_type=MESH,
        )

    def col_out_own(i, part):
        return pltpu.make_async_copy(
            col_out.at[which(part), pl.ds(i * COL_STEP, COL_STEP), pl.ds(xc * ROWS_HERE, ROWS_HERE)],
            raw_col.at[which(part), pl.ds(core * COL_BLOCK + i * COL_STEP, COL_STEP), :, lanes(x)],
            co_r.at[0],
        )

    class Side:
        pass

    def make_side(**fields):
        side = Side()
        for name, value in fields.items():
            setattr(side, name, value)
        return side

    def pair_copy(side, i, source):
        return pltpu.make_async_remote_copy(
            source.at[pl.ds(0, 2), pl.ds(i * side.step, side.step)],
            side.low.at[:, pl.ds(i * side.step, side.step)],
            side.f_s.at[0], side.f_r.at[i], device_id=side.partner, device_id_type=MESH,
        )

    def ahead_copy(i, a):
        return pltpu.make_async_remote_copy(
            inputs[a].at[pl.ds(i * ROW_STEP, ROW_STEP), :, lanes(y)],
            row_low.at[a, pl.ds(i * ROW_STEP, ROW_STEP), pl.ds(y * COLS_HERE, COLS_HERE)],
            rf_s.at[0], rf_r.at[i], device_id=row_partner, device_id_type=MESH,
        )

    def rest_copy(i, d):
        columns = pl.ds((y + d) % 4 * COLS_HERE, COLS_HERE)
        return pltpu.make_async_remote_copy(
            row_in.at[pl.ds(0, 2), pl.ds(i * ROW_STEP, ROW_STEP), columns],
            row_low.at[:, pl.ds(i * ROW_STEP, ROW_STEP), columns],
            rf_s.at[0], rf_r.at[i], device_id=row_partner, device_id_type=MESH,
        )

    def issue_row(i, pair):
        for a in (2 * pair, 2 * pair + 1):
            for d in (2, 1, 3):
                row_in_copy(i, a, d).start()
            row_in_own(i, a).start()

    def turn_blocks(part, pair):
        for a in (2 * pair, 2 * pair + 1):
            for core_of in range(2):
                stage_copy(a, part, core_of).wait()
                at = core_of * COL_BLOCK + part * 16
                send[a, pl.ds(at, 16)] = jnp.swapaxes(stage[a, :, pl.ds(at, 16), :], 0, 1)

    def issue_col(i, pair):
        for d in (4, 5, 2, 3, 6, 7, 1):
            col_in_copy(i, pair, d).start()
        col_in_own(i, pair).start()

    def issue(i, carry):
        for pair in range(2):
            issue_row(i, pair)
            issue_col(i, pair)
        return carry

    def send_row(i, part):
        for d in (2, 1, 3):
            row_out_copy(i, part, d).start()
        row_out_own(i, part).start()

    def send_col(i, part):
        for d in (4, 5, 2, 3, 6, 7, 1):
            col_out_copy(i, part, d).start()
        col_out_own(i, part).start()

    row_side = make_side(
        upper=z_hi == 1, step=ROW_STEP, unroll=ROW_UNROLL, length=ROW_SEQ, partner=row_partner,
        box=row_in, low=row_low, out=row_out, part=row_part, keep=row_keep, f_s=rf_s, f_r=rf_r,
        send=send_row,
    )
    col_side = make_side(
        upper=z_lo == 1, step=COL_STEP, unroll=COL_UNROLL, length=COL_SEQ, partner=col_partner,
        box=col_in, low=col_low, out=col_out, part=col_part, keep=col_keep, f_s=cf_s, f_r=cf_r,
        send=send_col,
    )

    def each(side, i, one):
        def some(m, carry):
            for u in range(side.unroll):
                one(i * side.step + m * side.unroll + u)
            return carry

        lax.fori_loop(0, side.step // side.unroll, some, 0)

    def bf16(value):
        return value.astype(jnp.bfloat16)

    def begin(side, i, upper):
        def lower_one(n):
            k, v, q, g = [side.box[a, n] for a in range(4)]
            found = attend(q, k, v, g)
            side.out[0, n] = found[0]
            side.out[1, n] = found[1]
            side.keep[0, n] = found[2]
            side.keep[1, n] = found[3]

        def upper_one(n):
            k, v, q, g = [side.box[a, n] for a in range(4)]
            found = attend(q, k, v, g, side.low[0, n], side.low[1, n])
            for a in range(4):
                side.out[a, n] = bf16(found[a])
            side.part[0, n] = bf16(found[4])
            side.part[1, n] = bf16(found[5])

        @pl.when(jnp.logical_not(side.upper) if not upper else side.upper)
        def _():
            if not upper:
                each(side, i, lower_one)
                side.send(i, 0)
                return
            pair_copy(side, i, side.part).wait_recv()
            each(side, i, upper_one)
            pair_copy(side, i, side.part).start()
            side.send(i, 2)

    def finish(side, i):
        def one(n):
            for a in range(2):
                side.out[2 + a, n] = bf16(side.keep[a, n] + side.low[a, n].astype(jnp.float32))

        @pl.when(jnp.logical_not(side.upper))
        def _():
            pair_copy(side, i, side.part).wait_recv()
            each(side, i, one)
            side.send(i, 1)

    def whole(ref, semaphore):
        pltpu.make_async_copy(ref, ref, semaphore).wait()

    def arrive_row(i, pair):
        whole(row_in.at[pl.ds(2 * pair, 2), pl.ds(i * ROW_STEP, ROW_STEP)], ri_r.at[i, pair])

    def arrive_col(i, pair):
        whole(col_in.at[pl.ds(2 * pair, 2), pl.ds(i * COL_STEP, COL_STEP)], ci_r.at[i, pair])

    def arrive(i, carry):
        arrive_row(i, 0)

        @pl.when(z_hi == 0)
        def _():
            @pl.when(i < ahead)
            def _():
                for d in range(1, 4):
                    rest_copy(i, d).start()

            @pl.when(i >= ahead)
            def _():
                pair_copy(row_side, i, row_in).start()

        arrive_col(i, 0)

        @pl.when(z_lo == 0)
        def _():
            pair_copy(col_side, i, col_in).start()

        arrive_row(i, 1)
        arrive_col(i, 1)
        return carry

    def stage_part(part):
        for a in range(4):
            for core_of in range(2):
                stage_copy(a, part, core_of).start()

    stage_part(0)
    turn_blocks(0, 0)
    pl.semaphore_wait(barrier, len(everyone))
    issue_row(0, 0)

    def send_ahead(i, carry):
        for a in range(2):
            ahead_copy(i, a).start()
        return carry

    ahead = jnp.where(z_lo == 0, FAR_AHEAD, AHEAD)

    @pl.when(z_hi == 0)
    def _():
        lax.fori_loop(0, ahead, send_ahead, 0)

    issue_col(0, 0)
    issue_row(0, 1)
    turn_blocks(0, 1)
    issue_col(0, 1)
    issue(1, 0)
    stage_part(1)
    arrive(0, 0)
    lax.fori_loop(2, 4, issue, 0)

    both_upper = jnp.logical_and(z_hi == 1, z_lo == 1)
    lag = jnp.where(z_hi + z_lo == 0, LONG_LAG, LAG)

    def until(i):
        return jnp.minimum(jnp.where(both_upper, i + 1, 2 * i + 3), STEPS)

    def step(i, carry):
        @pl.when(i == STEPS // 4 - 2)
        def _():
            turn_blocks(1, 0)
            turn_blocks(1, 1)

        lax.fori_loop(2 * i + 4, jnp.minimum(2 * i + 6, STEPS), issue, 0)
        lax.fori_loop(jnp.where(both_upper, jnp.maximum(i, 1), 2 * i + 1), until(i), arrive, 0)

        @pl.when(i < STEPS)
        def _():
            for upper in (False, True):
                for side in (row_side, col_side):
                    begin(side, i, upper)

        @pl.when(jnp.logical_and(i >= lag, i < STEPS + lag))
        def _():
            for side in (row_side, col_side):
                finish(side, i - lag)

        return carry

    lax.fori_loop(0, STEPS + LONG_LAG, step, 0)

    whole(row_in.at[pl.ds(0, 3)], ri_s.at[0])
    whole(col_in.at[:, pl.ds(0, COL_BLOCK * 7 // 8)], ci_s.at[0])
    for side in (row_side, col_side):
        whole(side.low, side.f_s.at[0])

    whole(row_out.at[pl.ds(0, 3)], ro_s.at[0])
    whole(col_out.at[:, pl.ds(0, COL_BLOCK * 7 // 8)], co_s.at[0])
    whole(raw_row, ro_r.at[0])
    whole(raw_col, co_r.at[0])


def exchange(queries, keys, values, grad_output):
    bf16, f32 = jnp.bfloat16, jnp.float32
    dma = pltpu.SemaphoreType.DMA

    def side(many, length):
        return [
            pltpu.VMEM((4, many, length, LANES), bf16),
            pltpu.VMEM((2, many, length, LANES), bf16),
            pltpu.VMEM((4, many, length, LANES), bf16),
            pltpu.VMEM((2, many, length, LANES), bf16),
            pltpu.VMEM((2, many, length, LANES), f32),
        ]

    return pl.pallas_call(
        body,
        out_shape=[
            jax.ShapeDtypeStruct((4, ROWS_HERE, COLS_HERE, HALF), bf16),
            jax.ShapeDtypeStruct((4, COLS_HERE, ROWS_HERE, HALF), bf16),
        ],
        in_specs=[pl.BlockSpec(memory_space=pl.ANY)] * 4,
        out_specs=[pl.BlockSpec(memory_space=pl.ANY)] * 2,
        scratch_shapes=side(ROWS_HERE, ROW_SEQ)
        + side(COL_BLOCK, COL_SEQ)
        + [pltpu.VMEM((4, ROWS_HERE, COLS_HERE, HALF), bf16), pltpu.VMEM((4, COLS_HERE, ROWS_HERE, HALF), bf16)]
        + [dma((1,)), dma((STEPS, 2)), dma((1,)), dma((STEPS, 2))]
        + [dma((1,))] * 4
        + [dma((1,)), dma((STEPS,))] * 2
        + [dma((4, 2, 2))],
        compiler_params=pltpu.CompilerParams(
            collective_id=0, has_side_effects=True, vmem_limit_bytes=60 * 2**20
        ),
        name="exchange",
    )(queries, keys, values, grad_output)


def join_body(row_ref, col_ref, out_0, out_1, out_2, out_3, rows, cols, turned, row_in, row_out, col_in, col_out):
    outs = (out_0, out_1, out_2, out_3)
    blocks = COLS_HERE // 16

    def load_row(a):
        return pltpu.make_async_copy(row_ref.at[a], rows.at[a], row_in.at[a])

    def store_row(a):
        return pltpu.make_async_copy(rows.at[a], outs[a].at[:, :, pl.ds(0, HALF)], row_out.at[a])

    def load_col(a, b):
        at = pl.ds(b * 16, 16)
        return pltpu.make_async_copy(col_ref.at[a, at], cols.at[a, at], col_in.at[a, b])

    def store_col(a, b):
        at = pl.ds(b * 16, 16)
        return pltpu.make_async_copy(turned.at[a, :, at], outs[a].at[:, at, pl.ds(HALF, HALF)], col_out.at[a, b])

    for a in range(4):
        for b in range(blocks):
            load_col(a, b).start()
        load_row(a).start()
    for a in range(4):
        for b in range(blocks):
            load_col(a, b).wait()
            at = pl.ds(b * 16, 16)
            turned[a, :, at] = jnp.swapaxes(cols[a, at], 0, 1)
            store_col(a, b).start()
        load_row(a).wait()
        store_row(a).start()
    for a in range(4):
        for b in range(blocks):
            store_col(a, b).wait()
        store_row(a).wait()


def join(raw_row, raw_col):
    shape = jax.ShapeDtypeStruct((ROWS_HERE, COLS_HERE, 2 * HALF), jnp.bfloat16)
    dma = pltpu.SemaphoreType.DMA
    return pl.pallas_call(
        join_body,
        out_shape=[shape] * 4,
        in_specs=[pl.BlockSpec(memory_space=pl.ANY)] * 2,
        out_specs=[pl.BlockSpec(memory_space=pl.ANY)] * 4,
        scratch_shapes=[
            pltpu.VMEM((4, ROWS_HERE, COLS_HERE, HALF), jnp.bfloat16),
            pltpu.VMEM((4, COLS_HERE, ROWS_HERE, HALF), jnp.bfloat16),
            pltpu.VMEM((4, ROWS_HERE, COLS_HERE, HALF), jnp.bfloat16),
            dma((4,)), dma((4,)), dma((4, COLS_HERE // 16)), dma((4, COLS_HERE // 16)),
        ],
        compiler_params=pltpu.CompilerParams(vmem_limit_bytes=62 * 2**20),
        name="join",
    )(raw_row, raw_col)


def on_device(queries, keys, values, grad_output):
    raw_row, raw_col = exchange(queries, keys, values, grad_output)
    return tuple(join(raw_row, raw_col))


def solution(mesh):
    spec = P("row", "col", None)
    return jax.shard_map(
        on_device, mesh=mesh, in_specs=(spec,) * 4, out_specs=(spec,) * 4, check_vma=False
    )
```
